32 devices in a mesh: pipe: 4 (over z), ctx: 8 (over y, x, core).
Axes of the slice: x: 2, y: 2, z: 4, core: 2. Of those that a mesh axis runs over, the one named last changes fastest.
Arguments:
- queries: bfloat16 [4, 3072, 4096], P('pipe', 'ctx'), may hold values from -1.796875 to 1.796875
- key_rows: bfloat16 [4, 3072, 4096], P('pipe', 'ctx'), may hold values from -1.796875 to 1.796875
- value_rows: bfloat16 [4, 3072, 4096], P('pipe', 'ctx'), may hold values from -6 to 6
- next_grads: bfloat16 [4, 3072, 4096], P('pipe', 'ctx'), may hold values from -0.29882812 to 0.29882812
- log_decay: float32 [4, 32, 3072], P('pipe', None, 'ctx'), may hold values from -1.5 to 0, as said below
- doc_ids: int32 [4, 3072], P('pipe', 'ctx'), may hold values from 0 to 3, never falling along the last dimension, each value on 1 to 1536 neighbouring positions
- prefix_states: float32 [4, 8, 32, 128, 128], P('pipe', 'ctx'), may hold values from -24 to 24
Outputs:
- grad_q: bfloat16 [4, 3072, 4096], P('pipe', 'ctx')
- grad_k: bfloat16 [4, 3072, 4096], P('pipe', 'ctx')
- grad_v: bfloat16 [4, 3072, 4096], P('pipe', 'ctx')
The draws below stay inside these ranges and needn't reach their ends.
Inputs may be any that keep to these rules, and one draw needn't show every extreme that they name: `doc_ids`: in each section ids never fall along the sequence; each of the 4 documents holds 1 to 1536 tokens, one exactly 1536. `log_decay`: every entry is negative.
All inputs are finite; a program needn't handle non-finite values.
Results may differ from the reference program's by a relative error of at most 0.0053.
Values may be sent and summed in bfloat16 or wider, within the bound.
A program may use at most 192 MiB of HBM per device.

```python
import math
import jax
import jax.numpy as jnp
import numpy as np
from jax import lax

HEAD_TOTAL = 32
HEAD_DIM = 128
TOK_DEV = 384
DOCS = 4
SECTION_TOTAL = 4
SECTION_TOKENS = 3072
HD = 4096
N_CTX = 8


def draw_log_decay(key, part):
    parallel_flows = jax.random.split(key, 8)
    fast_share = 0.5
    token_factor = jnp.exp(jax.random.uniform(parallel_flows[5], (SECTION_TOTAL, HEAD_TOTAL, SECTION_TOKENS), jnp.float32, math.log(0.5), math.log(2.0)))
    fast_head = jax.random.uniform(parallel_flows[0], (SECTION_TOTAL, HEAD_TOTAL, 1), jnp.float32) < fast_share
    fast_rate = jnp.exp(jax.random.uniform(parallel_flows[1], (SECTION_TOTAL, HEAD_TOTAL, 1), jnp.float32, math.log(1.0 / 40.0), math.log(1.0 / 10.0)))
    slow_rate = jnp.exp(jax.random.uniform(parallel_flows[2], (SECTION_TOTAL, HEAD_TOTAL, 1), jnp.float32, math.log(0.05), math.log(0.4))) / SECTION_TOKENS
    base_rate = jnp.where(fast_head, fast_rate, slow_rate)
    block_factor = jnp.exp(jax.random.uniform(parallel_flows[3], (SECTION_TOTAL, HEAD_TOTAL, SECTION_TOKENS // TOK_DEV, 1), jnp.float32, math.log(0.005), math.log(2.0)))
    block_factor = jnp.broadcast_to(block_factor, (SECTION_TOTAL, HEAD_TOTAL, SECTION_TOKENS // TOK_DEV, TOK_DEV)).reshape(SECTION_TOTAL, HEAD_TOTAL, SECTION_TOKENS)
    piece_count = (SECTION_TOKENS + 63) // 64
    piece_factor = jnp.exp(jax.random.uniform(parallel_flows[7], (SECTION_TOTAL, HEAD_TOTAL, piece_count, 1), jnp.float32, math.log(0.01), math.log(3.0)))
    piece_factor = jnp.broadcast_to(piece_factor, (SECTION_TOTAL, HEAD_TOTAL, piece_count, 64)).reshape(SECTION_TOTAL, HEAD_TOTAL, piece_count * 64)[:, :, :SECTION_TOKENS]
    gentle_portion = -base_rate * block_factor * piece_factor * token_factor
    sudden_location = jax.random.randint(parallel_flows[4], (SECTION_TOTAL, 2, 1), 0, SECTION_TOKENS)
    sudden_hit = jnp.where(jnp.arange(SECTION_TOKENS)[None, None, :] == sudden_location, 1.0, 0.0)
    sudden_keep = jnp.log(jax.random.uniform(parallel_flows[6], (SECTION_TOTAL, 2, HEAD_TOTAL), jnp.float32, 0.6, 0.8))
    sudden_portion = jnp.einsum('knx,knu->kxu', sudden_keep, sudden_hit)
    return jnp.maximum(gentle_portion + sudden_portion, -1.5).astype(jnp.float32)


def shard_levels(key, dims, cuts, smallest, high):
    def one(dim, parts):
        steps = jax.random.uniform(jax.random.fold_in(jax.random.fold_in(key, 6), dim), (parts,), jnp.float32, smallest / len(cuts), high / len(cuts))
        return jnp.repeat(jnp.exp(steps), dims[dim] // parts).reshape((-1,) + (1,) * (len(dims) - dim - 1))

    gain = one(*cuts[0])
    for cut in cuts[1:]:
        gain = gain * one(*cut)
    return gain


def length_profile(amount, total, limit, lean):
    portions = [(1 << 20) // math.isqrt(standing ** lean) + 1 for standing in range(2, amount + 1)]
    spare, counts = total - limit - (amount - 1), [1] * (amount - 1)
    while spare > 0:
        movable = [i for i in range(amount - 1) if counts[i] < limit]
        mass, budget = sum([portions[i] for i in movable]), spare
        for i in movable:
            more = min(limit - counts[i], max(1, budget * portions[i] // mass), spare)
            counts[i] = counts[i] + more
            spare = spare - more
    return np.array([limit] + counts)


def ragged_sizes(key, count, total, bound, lean):
    if count == 2:
        one = jax.random.randint(key, (), max(1, total - bound), min(bound, total - 1) + 1)
        return jnp.stack([one, total - one])
    tallies = jnp.asarray(length_profile(count, total, bound, lean), jnp.int32)
    twos = (count - 1) // 2
    donor, receiver = tallies[1:1 + 2 * twos:2], tallies[2:2 + 2 * twos:2]
    margin = jnp.minimum(donor - 1, bound - receiver)
    shifted = jax.random.randint(jax.random.fold_in(key, 1), (twos,), 0, 1 << 20) % (margin + 1)
    tallies = tallies.at[1:1 + 2 * twos:2].set(donor - shifted).at[2:2 + 2 * twos:2].set(receiver + shifted)
    return tallies[jax.random.permutation(jax.random.fold_in(key, 2), count)]


def gaussian(own_key, shape, scale, limit, cuts=(), held_as=jnp.bfloat16):
    array = scale * jax.random.normal(own_key, shape, jnp.float32)
    if cuts:
        array = array * shard_levels(own_key, shape, cuts, -0.22, 0.18)
    return jnp.clip(array, -limit, limit).astype(held_as)


def setup_inputs(seed: int = 0) -> dict:
    streams_of = jax.random.split(jax.random.key(seed), 8)
    return {
        "queries": gaussian(streams_of[0], (SECTION_TOTAL, SECTION_TOKENS, HD), 0.3, 1.796875, ((0, 4), (1, 8))),
        "key_rows": gaussian(streams_of[1], (SECTION_TOTAL, SECTION_TOKENS, HD), 0.3, 1.796875, ((0, 4), (1, 8))),
        "value_rows": gaussian(streams_of[2], (SECTION_TOTAL, SECTION_TOKENS, HD), 1.0, 6.0, ((0, 4), (1, 8))),
        "next_grads": gaussian(streams_of[3], (SECTION_TOTAL, SECTION_TOKENS, HD), 0.05, 0.29882812, ((0, 4), (1, 8))),
        "log_decay": draw_log_decay(jax.random.fold_in(streams_of[7], 71), 0),
        "doc_ids": jax.vmap(lambda own: jnp.searchsorted(jnp.cumsum(ragged_sizes(own, DOCS, SECTION_TOKENS, SECTION_TOKENS // 2, 0)), jnp.arange(SECTION_TOKENS), side="right"))(jax.random.split(streams_of[5], SECTION_TOTAL)).reshape((SECTION_TOTAL, SECTION_TOKENS)).astype(jnp.int32),
        "prefix_states": gaussian(streams_of[6], (SECTION_TOTAL, N_CTX, HEAD_TOTAL, HEAD_DIM, HEAD_DIM), 4.0, 24.0, ((0, 4), (1, 8)), jnp.float32),
    }


def local_block(queries, key_rows, value_rows, grad_rows, log_decay, doc_ids, prefix_state, prior_last):
    head_count = log_decay.shape[0]
    length = queries.shape[0]
    head_dim = queries.shape[1] // head_count
    query_heads = queries.reshape(length, head_count, head_dim).astype(jnp.float32)
    key_heads = key_rows.reshape(length, head_count, head_dim).astype(jnp.float32)
    value_heads = value_rows.reshape(length, head_count, head_dim).astype(jnp.float32)
    grad_heads = grad_rows.reshape(length, head_count, head_dim).astype(jnp.float32)
    running = jnp.cumsum(log_decay, axis=1)
    block_total = running[:, -1]
    position = jnp.arange(length)
    same_doc = (doc_ids[:, None] == doc_ids[None, :]) & (position[None, :] <= position[:, None])
    spread = running[:, :, None] - running[:, None, :]
    weight = jnp.where(same_doc[None], jnp.exp(jnp.where(same_doc[None], spread, 0.0)), 0.0)
    scores = jnp.einsum("ihd,jhd->hij", query_heads, key_heads)
    attention = lax.optimization_barrier((weight * scores).astype(jnp.bfloat16)).astype(jnp.float32)
    grad_dots = jnp.einsum("ihd,jhd->hij", grad_heads, value_heads)
    grad_mix = lax.optimization_barrier((weight * grad_dots).astype(jnp.bfloat16)).astype(jnp.float32)
    continues = prior_last == doc_ids[0] + 1
    head_mask = jnp.where((doc_ids == doc_ids[0]) & continues, 1.0, 0.0)
    head_weight = jnp.exp(running).T * head_mask[:, None]
    weighted = lax.optimization_barrier((head_weight[:, :, None] * grad_heads).astype(jnp.bfloat16)).astype(jnp.float32)
    head_state = jnp.einsum("ihd,ihe->hde", query_heads, weighted)
    carry_link = jnp.where((doc_ids[0] == doc_ids[-1]) & continues, jnp.exp(block_total), 0.0)
    prefix_low = lax.optimization_barrier(prefix_state.astype(jnp.bfloat16)).astype(jnp.float32)
    grad_prefix = jnp.einsum("hde,ihe->ihd", prefix_low, grad_heads) * head_weight[:, :, None]
    grad_query = (jnp.einsum("hij,jhd->ihd", grad_mix, key_heads) + grad_prefix).astype(jnp.bfloat16)
    key_inner = jnp.einsum("hij,ihd->jhd", grad_mix, query_heads)
    value_inner = jnp.einsum("hij,ihd->jhd", attention, grad_heads)
    tail_mask = (doc_ids == doc_ids[-1])[None, :]
    tail_weight = jnp.where(tail_mask, jnp.exp(jnp.where(tail_mask, block_total[:, None] - running, 0.0)), 0.0).T
    return grad_query.reshape(length, -1), key_inner, value_inner, head_state, carry_link, tail_weight


def finish_block(key_inner, value_inner, suffix, tail_weight, key_rows, value_rows):
    length = key_rows.shape[0]
    head_count = suffix.shape[0]
    head_dim = suffix.shape[1]
    key_heads = key_rows.reshape(length, head_count, head_dim).astype(jnp.float32)
    value_heads = value_rows.reshape(length, head_count, head_dim).astype(jnp.float32)
    suffix_low = lax.optimization_barrier(suffix.astype(jnp.bfloat16)).astype(jnp.float32)
    grad_key = key_inner + jnp.einsum("hde,jhe->jhd", suffix_low, value_heads) * tail_weight[:, :, None]
    grad_value = value_inner + jnp.einsum("hde,jhd->jhe", suffix_low, key_heads) * tail_weight[:, :, None]
    return grad_key.astype(jnp.bfloat16).reshape(length, -1), grad_value.astype(jnp.bfloat16).reshape(length, -1)


def reference(queries, key_rows, value_rows, next_grads, log_decay, doc_ids, prefix_states):
    query_list, key_list, value_list = [], [], []
    for section in range(SECTION_TOTAL):
        out_grads = next_grads[(section + 1) % SECTION_TOTAL]
        doc_row = doc_ids[section]
        block_last = doc_row[TOK_DEV - 1::TOK_DEV]
        prior = jnp.concatenate([jnp.zeros((1,), jnp.int32), (block_last[:-1] + 1).astype(jnp.int32)])
        width = queries.shape[2]
        heads_here = log_decay.shape[1]
        query_blocks = queries[section].reshape(N_CTX, TOK_DEV, width)
        key_blocks = key_rows[section].reshape(N_CTX, TOK_DEV, width)
        value_blocks = value_rows[section].reshape(N_CTX, TOK_DEV, width)
        grad_blocks = out_grads.reshape(N_CTX, TOK_DEV, width)
        decay_blocks = jnp.transpose(log_decay[section].reshape(heads_here, N_CTX, TOK_DEV), (1, 0, 2))
        doc_blocks = doc_row.reshape(N_CTX, TOK_DEV)

        def run_local(packed):
            return local_block(*packed)

        grad_query, key_inner, value_inner, head_state, carry_link, tail_weight = lax.map(
            run_local, (query_blocks, key_blocks, value_blocks, grad_blocks, decay_blocks, doc_blocks,
                        prefix_states[section], prior))

        def chain_step(carry_state, element):
            link_now, state_now = element
            return state_now + link_now[:, None, None] * carry_state, carry_state

        final_state, suffix = lax.scan(chain_step, jnp.zeros_like(head_state[0]), (carry_link, head_state), reverse=True)

        def run_finish(packed):
            return finish_block(*packed)

        grad_key, grad_value = lax.map(run_finish, (key_inner, value_inner, suffix, tail_weight, key_blocks, value_blocks))
        query_list.append(grad_query.reshape(SECTION_TOKENS, width))
        key_list.append(grad_key.reshape(SECTION_TOKENS, width))
        value_list.append(grad_value.reshape(SECTION_TOKENS, width))
    return jnp.stack(query_list), jnp.stack(key_list), jnp.stack(value_list)
```

```python
import functools

import jax
import jax.numpy as jnp
from jax import lax
from jax.experimental import pallas as pl
from jax.experimental.pallas import tpu as pltpu
from jax.sharding import PartitionSpec as P

MESH = pl.DeviceIdType.MESH
LANES = 128
CHUNK_HEADS = 2
IN_FLIGHT = 4
MASKED = -1e30


def dot(a, b, a_dim, b_dim, precision=None):
    return lax.dot_general(
        a,
        b,
        (((a_dim,), (b_dim,)), ((), ())),
        precision=precision,
        preferred_element_type=jnp.float32,
    )


def as_columns(row, width):
    return jnp.broadcast_to(row, (width, row.shape[1])).T


def kernel(
    pipe_count,
    ctx_count,
    q_hbm,
    k_hbm,
    v_hbm,
    g_hbm,
    decay_ref,
    doc_ref,
    prefix_hbm,
    out_q,
    out_k,
    out_v,
    q_s,
    k_s,
    v_s,
    g_s,
    prefix_s,
    run_s,
    col_s,
    bias_s,
    head_mask_s,
    tail_mask_s,
    meta_own,
    meta_all,
    link_s,
    cont_s,
    state_s,
    odd_state_s,
    pair_s,
    pair_in_s,
    odd_suffix_s,
    suffix_in_s,
    load_sem,
    prefix_sem,
    store_sem,
    g_send,
    g_recv,
    meta_send,
    meta_recv,
    state_send,
    state_recv,
    pair_send,
    pair_recv,
    suffix_send,
    suffix_recv,
):
    chunks, length, chunk_cols = q_s.shape
    head_dim = chunk_cols // CHUNK_HEADS
    heads = run_s.shape[0]
    blocks = length // LANES
    pairs = ctx_count // 2
    reach = ctx_count // 4
    section = lax.axis_index("pipe")
    me = lax.axis_index("ctx")
    odd = lax.rem(me, 2)
    pair = me // 2
    earlier = lax.rem(section + pipe_count - 1, pipe_count)
    later = lax.rem(section + 1, pipe_count)

    barrier = pltpu.get_barrier_semaphore()
    pl.semaphore_signal(barrier, inc=1, device_id={"pipe": earlier}, device_id_type=MESH)
    pl.semaphore_signal(barrier, inc=1, device_id={"pipe": later}, device_id_type=MESH)
    for k in range(1, ctx_count):
        pl.semaphore_signal(
            barrier, inc=1, device_id={"ctx": lax.rem(me + k, ctx_count)}, device_id_type=MESH
        )
    pl.semaphore_wait(barrier, ctx_count + 1)

    def columns(t):
        return pl.ds(pl.multiple_of(t * chunk_cols, chunk_cols), chunk_cols)

    def grad_copy(t):
        return pltpu.make_async_remote_copy(
            src_ref=g_hbm.at[0, :, columns(t)],
            dst_ref=g_s.at[t],
            send_sem=g_send.at[t],
            recv_sem=g_recv.at[t],
            device_id={"pipe": earlier},
            device_id_type=MESH,
        )

    def load_copy(i, t):
        source, target = ((q_hbm, q_s), (k_hbm, k_s), (v_hbm, v_s))[i]
        return pltpu.make_async_copy(
            source.at[0, :, columns(t)], target.at[t], load_sem.at[i, t]
        )

    def store_copy(i, t):
        source, target = ((q_s, out_q), (k_s, out_k), (v_s, out_v))[i]
        return pltpu.make_async_copy(
            source.at[t], target.at[0, :, columns(t)], store_sem.at[i, t]
        )

    def meta_copy(k):
        return pltpu.make_async_remote_copy(
            src_ref=meta_own,
            dst_ref=meta_all.at[me],
            send_sem=meta_send.at[k],
            recv_sem=meta_recv.at[k],
            device_id={"ctx": lax.rem(me + k, ctx_count)},
            device_id_type=MESH,
        )

    def meta_arrival(k):
        return pltpu.make_async_remote_copy(
            src_ref=meta_own,
            dst_ref=meta_all.at[lax.rem(me + ctx_count - k, ctx_count)],
            send_sem=meta_send.at[k],
            recv_sem=meta_recv.at[k],
            device_id={"ctx": lax.rem(me + k, ctx_count)},
            device_id_type=MESH,
        )

    partner = me + 1 - 2 * odd

    def state_copy(t):
        return pltpu.make_async_remote_copy(
            src_ref=state_s.at[t],
            dst_ref=odd_state_s.at[t],
            send_sem=state_send.at[t],
            recv_sem=state_recv.at[t],
            device_id={"ctx": partner},
            device_id_type=MESH,
        )

    def suffix_copy(t):
        return pltpu.make_async_remote_copy(
            src_ref=odd_suffix_s.at[t],
            dst_ref=suffix_in_s.at[t],
            send_sem=suffix_send.at[t],
            recv_sem=suffix_recv.at[t],
            device_id={"ctx": partner},
            device_id_type=MESH,
        )

    def pair_copy(d, t):
        return pltpu.make_async_remote_copy(
            src_ref=pair_s.at[t],
            dst_ref=pair_in_s.at[d - 1, t],
            send_sem=pair_send.at[d - 1, t],
            recv_sem=pair_recv.at[d - 1, t],
            device_id={"ctx": lax.rem(me - 2 * d + 1 + ctx_count, ctx_count)},
            device_id_type=MESH,
        )

    for t in range(IN_FLIGHT):
        grad_copy(t).start()

    @pl.loop(0, chunks)
    def _(t):
        for i in range(3):
            load_copy(i, t).start()

    prefix_copy = pltpu.make_async_copy(prefix_hbm.at[0, 0], prefix_s, prefix_sem)
    prefix_copy.start()

    rows = lax.broadcasted_iota(jnp.int32, (length, length), 0)
    cols = lax.broadcasted_iota(jnp.int32, (length, length), 1)
    ordered = rows <= cols
    running = dot(
        decay_ref[0], jnp.where(ordered, 1.0, 0.0), 1, 0, precision=lax.Precision.HIGHEST
    )
    run_s[...] = running
    doc_row = doc_ref[...].astype(jnp.float32)
    first_doc = jnp.broadcast_to(doc_row[:, 0:1], (8, LANES))
    last_doc = jnp.broadcast_to(doc_row[:, length - 1 : length], (8, LANES))
    meta_own[0:heads] = jnp.broadcast_to(
        jnp.exp(running[:, length - 1 : length]), (heads, LANES)
    )
    meta_own[heads : heads + 8] = first_doc
    meta_own[heads + 8 : heads + 16] = last_doc
    meta_all[me] = meta_own[...]
    for k in range(1, ctx_count):
        meta_copy(k).start()

    doc_cols = as_columns(doc_row, LANES)
    doc_wide = jnp.concatenate([doc_cols] * blocks, axis=1)
    bias_s[...] = jnp.where(ordered & (doc_wide == doc_row), 0.0, MASKED)
    tail_mask_s[...] = jnp.where(doc_cols == last_doc[0:1], 1.0, 0.0)

    @pl.loop(0, heads)
    def _(h):
        col_s[h] = as_columns(run_s[pl.ds(h, 1), :], LANES)

    for k in range(1, ctx_count):
        meta_arrival(k).wait_recv()
    for b in range(ctx_count):
        first_here = meta_all[b, heads : heads + 8]
        last_here = meta_all[b, heads + 8 : heads + 16]
        if b > 0:
            last_before = meta_all[b - 1, heads + 8 : heads + 16]
            continues = jnp.where(first_here == last_before, 1.0, 0.0)
        else:
            continues = jnp.zeros((8, LANES), jnp.float32)
        cont_s[b] = continues
        passes = jnp.where(first_here == last_here, continues, 0.0)
        link_s[b] = meta_all[b, 0:heads] * passes[0:1]
    head_mask_s[...] = jnp.where(doc_cols == first_doc[0:1], 1.0, 0.0) * cont_s[me][0:1]
    prefix_copy.wait()

    def part(u):
        return slice(u * head_dim, (u + 1) * head_dim)

    def head_weight(h):
        return jnp.exp(col_s[h]) * head_mask_s[...]

    def stage_state(t):
        grad_copy(t).wait_recv()
        load_copy(0, t).wait()
        for u in range(CHUNK_HEADS):
            weighted = head_weight(t * CHUNK_HEADS + u) * g_s[t, :, part(u)].astype(jnp.float32)
            state_s[t, u] = dot(q_s[t, :, part(u)], weighted.astype(jnp.bfloat16), 0, 0)

        @pl.when(odd == 1)
        def _():
            state_copy(t).start()

        grad_copy(t).wait_send()

        @pl.when(t + IN_FLIGHT < chunks)
        def _():
            grad_copy(t + IN_FLIGHT).start()

    def stage_pair(t):
        state_copy(t).wait_recv()
        for u in range(CHUNK_HEADS):
            link = link_s[me, pl.ds(t * CHUNK_HEADS + u, 1), :]
            pair_s[t, u] = state_s[t, u] + link * odd_state_s[t, u]
        for d in range(1, reach + 1):

            @pl.when(pair >= d)
            def _():
                pair_copy(d, t).start()

    def stage_suffix(t):
        odd_suffix_s[t] = jnp.zeros(odd_suffix_s.shape[1:], jnp.float32)
        for d in range(1, reach + 1):

            @pl.when(pair + d < pairs)
            def _():
                pair_copy(d, t).wait_recv()
                for u in range(CHUNK_HEADS):
                    term = pair_in_s[d - 1, t, u]
                    for b in range(1, 2 * d - 1):
                        term = term * link_s[me + b, pl.ds(t * CHUNK_HEADS + u, 1), :]
                    odd_suffix_s[t, u] += term

        suffix_copy(t).start()

    def stage_grads(t):
        load_copy(1, t).wait()
        load_copy(2, t).wait()

        @pl.when(odd == 0)
        def _():
            suffix_copy(t).wait_recv()
            for u in range(CHUNK_HEADS):
                link = link_s[me + 1, pl.ds(t * CHUNK_HEADS + u, 1), :]
                odd_suffix_s[t, u] = odd_state_s[t, u] + link * suffix_in_s[t, u]

        for u in range(CHUNK_HEADS):
            h = t * CHUNK_HEADS + u
            q, k, v, g = (ref[t, :, part(u)] for ref in (q_s, k_s, v_s, g_s))
            suffix = odd_suffix_s[t, u].astype(jnp.bfloat16)
            prefix = prefix_s[h].astype(jnp.bfloat16)
            grad_q = [None] * blocks
            total = col_s[h, length - 1 : length, :]
            row = run_s[pl.ds(h, 1), :]
            for block in range(blocks):
                low, high = block * LANES, (block + 1) * LANES
                col = col_s[h, low:high, :]
                wide = jnp.concatenate([col] * (blocks - block), axis=1)
                weight = jnp.exp((row[:, low:] - wide) + bias_s[low:high, low:])
                scores = dot(k[low:high], q[low:], 1, 1)
                grad_dots = dot(v[low:high], g[low:], 1, 1)
                attention = (weight * scores).astype(jnp.bfloat16)
                grad_mix = (weight * grad_dots).astype(jnp.bfloat16)
                tail = jnp.exp(total - col) * tail_mask_s[low:high]
                grad_k = dot(grad_mix, q[low:], 1, 0) + dot(v[low:high], suffix, 1, 1) * tail
                grad_v = dot(attention, g[low:], 1, 0) + dot(k[low:high], suffix, 1, 0) * tail
                spread = dot(grad_mix, k[low:high], 0, 0)
                for i in range(block, blocks):
                    piece = spread[(i - block) * LANES : (i - block + 1) * LANES]
                    grad_q[i] = piece if grad_q[i] is None else grad_q[i] + piece
                k_s[t, low:high, part(u)] = grad_k.astype(jnp.bfloat16)
                v_s[t, low:high, part(u)] = grad_v.astype(jnp.bfloat16)
            grad_q = jnp.concatenate(grad_q, axis=0) + dot(g, prefix, 1, 1) * head_weight(h)
            q_s[t, :, part(u)] = grad_q.astype(jnp.bfloat16)
        for i in range(3):
            store_copy(i, t).start()

    @pl.loop(0, chunks + 3)
    def _(step):
        @pl.when(step < chunks)
        def _():
            stage_state(step)

        @pl.when((step >= 1) & (step < chunks + 1) & (odd == 0))
        def _():
            stage_pair(step - 1)

        @pl.when((step >= 2) & (step < chunks + 2) & (odd == 1))
        def _():
            stage_suffix(step - 2)

        @pl.when(step >= 3)
        def _():
            stage_grads(step - 3)

    for k in range(1, ctx_count):
        meta_copy(k).wait_send()

    @pl.loop(0, chunks)
    def _(t):
        for i in range(3):
            store_copy(i, t).wait()

        @pl.when(odd == 1)
        def _():
            state_copy(t).wait_send()
            suffix_copy(t).wait_send()

        for d in range(1, reach + 1):

            @pl.when((odd == 0) & (pair >= d))
            def _():
                pair_copy(d, t).wait_send()


def solution(mesh):
    pipe_count, ctx_count = mesh.shape["pipe"], mesh.shape["ctx"]

    def on_device(queries, key_rows, value_rows, next_grads, log_decay, doc_ids, prefix_states):
        _, length, width = queries.shape
        heads = log_decay.shape[1]
        head_dim = width // heads
        chunks = heads // CHUNK_HEADS
        chunk_cols = head_dim * CHUNK_HEADS
        reach = ctx_count // 4
        any_spec = pl.BlockSpec(memory_space=pl.ANY)
        vmem_spec = pl.BlockSpec(memory_space=pltpu.VMEM)
        f32, bf16 = jnp.float32, jnp.bfloat16
        rows = pltpu.VMEM((chunks, length, chunk_cols), bf16)
        states = pltpu.VMEM((chunks, CHUNK_HEADS, head_dim, head_dim), f32)
        mask = pltpu.VMEM((length, LANES), f32)
        dma = pltpu.SemaphoreType.DMA
        return pl.pallas_call(
            functools.partial(kernel, pipe_count, ctx_count),
            out_shape=[jax.ShapeDtypeStruct(queries.shape, bf16)] * 3,
            in_specs=[any_spec] * 4 + [vmem_spec] * 2 + [any_spec],
            out_specs=[any_spec] * 3,
            scratch_shapes=[
                rows,
                rows,
                rows,
                rows,
                pltpu.VMEM((heads, head_dim, head_dim), f32),
                pltpu.VMEM((heads, length), f32),
                pltpu.VMEM((heads, length, LANES), f32),
                pltpu.VMEM((length, length), f32),
                mask,
                mask,
                pltpu.VMEM((heads + 16, LANES), f32),
                pltpu.VMEM((ctx_count, heads + 16, LANES), f32),
                pltpu.VMEM((ctx_count, heads, LANES), f32),
                pltpu.VMEM((ctx_count, 8, LANES), f32),
                states,
                states,
                states,
                pltpu.VMEM((reach, chunks, CHUNK_HEADS, head_dim, head_dim), f32),
                states,
                states,
                dma((3, chunks)),
                dma,
                dma((3, chunks)),
                dma((chunks,)),
                dma((chunks,)),
                dma((ctx_count,)),
                dma((ctx_count,)),
                dma((chunks,)),
                dma((chunks,)),
                dma((reach, chunks)),
                dma((reach, chunks)),
                dma((chunks,)),
                dma((chunks,)),
            ],
            compiler_params=pltpu.CompilerParams(
                collective_id=0, has_side_effects=True, vmem_limit_bytes=56 * 1024 * 1024
            ),
        )(queries, key_rows, value_rows, next_grads, log_decay, doc_ids, prefix_states)

    return jax.shard_map(
        on_device,
        mesh=mesh,
        in_specs=(
            P("pipe", "ctx", None),
            P("pipe", "ctx", None),
            P("pipe", "ctx", None),
            P("pipe", "ctx", None),
            P("pipe", None, "ctx"),
            P("pipe", "ctx"),
            P("pipe", "ctx", None, None, None),
        ),
        out_specs=(P("pipe", "ctx", None), P("pipe", "ctx", None), P("pipe", "ctx", None)),
        check_vma=False,
    )
```

```python
import functools

import jax
import jax.numpy as jnp
from jax import lax
from jax.experimental import pallas as pl
from jax.experimental.pallas import tpu as pltpu
from jax.sharding import PartitionSpec as P

MESH = pl.DeviceIdType.MESH
LANES = 128
CHUNK_HEADS = 2
IN_FLIGHT = 4
SLOTS = 3
MASKED = -1e30


def dot(a, b, a_dim, b_dim, precision=None):
    return lax.dot_general(
        a,
        b,
        (((a_dim,), (b_dim,)), ((), ())),
        precision=precision,
        preferred_element_type=jnp.float32,
    )


def as_columns(row, width):
    return jnp.broadcast_to(row, (width, row.shape[1])).T


def kernel(
    pipe_count,
    ctx_count,
    q_hbm,
    k_hbm,
    v_hbm,
    g_hbm,
    decay_ref,
    doc_ref,
    prefix_hbm,
    out_q,
    out_k,
    out_v,
    q_s,
    k_s,
    v_s,
    g_s,
    prefix_s,
    run_s,
    col_s,
    bias_s,
    head_mask_s,
    tail_mask_s,
    meta_own,
    meta_all,
    link_s,
    cont_s,
    state_s,
    odd_state_s,
    pair_s,
    pair_in_s,
    odd_suffix_s,
    suffix_in_s,
    inner_s,
    load_sem,
    prefix_sem,
    g_send,
    g_recv,
    meta_send,
    meta_recv,
    state_send,
    state_recv,
    pair_send,
    pair_recv,
    suffix_send,
    suffix_recv,
):
    chunks, length, chunk_cols = q_s.shape
    head_dim = chunk_cols // CHUNK_HEADS
    heads = run_s.shape[0]
    blocks = length // LANES
    pairs = ctx_count // 2
    reach = ctx_count // 4
    section = lax.axis_index("pipe")
    me = lax.axis_index("ctx")
    odd = lax.rem(me, 2)
    pair = me // 2
    earlier = lax.rem(section + pipe_count - 1, pipe_count)
    later = lax.rem(section + 1, pipe_count)

    barrier = pltpu.get_barrier_semaphore()
    pl.semaphore_signal(barrier, inc=1, device_id={"pipe": earlier}, device_id_type=MESH)
    pl.semaphore_signal(barrier, inc=1, device_id={"pipe": later}, device_id_type=MESH)
    for k in range(1, ctx_count):
        pl.semaphore_signal(
            barrier, inc=1, device_id={"ctx": lax.rem(me + k, ctx_count)}, device_id_type=MESH
        )
    pl.semaphore_wait(barrier, ctx_count + 1)

    def columns(t):
        return pl.ds(pl.multiple_of(t * chunk_cols, chunk_cols), chunk_cols)

    def grad_copy(t):
        return pltpu.make_async_remote_copy(
            src_ref=g_hbm.at[0, :, columns(t)],
            dst_ref=g_s.at[t],
            send_sem=g_send.at[t],
            recv_sem=g_recv.at[t],
            device_id={"pipe": earlier},
            device_id_type=MESH,
        )

    def load_copy(i, t):
        source, target = ((q_hbm, q_s), (k_hbm, k_s), (v_hbm, v_s))[i]
        return pltpu.make_async_copy(
            source.at[0, :, columns(t)], target.at[t], load_sem.at[i, t]
        )

    def meta_copy(k):
        return pltpu.make_async_remote_copy(
            src_ref=meta_own,
            dst_ref=meta_all.at[me],
            send_sem=meta_send.at[k],
            recv_sem=meta_recv.at[k],
            device_id={"ctx": lax.rem(me + k, ctx_count)},
            device_id_type=MESH,
        )

    def meta_arrival(k):
        return pltpu.make_async_remote_copy(
            src_ref=meta_own,
            dst_ref=meta_all.at[lax.rem(me + ctx_count - k, ctx_count)],
            send_sem=meta_send.at[k],
            recv_sem=meta_recv.at[k],
            device_id={"ctx": lax.rem(me + k, ctx_count)},
            device_id_type=MESH,
        )

    partner = me + 1 - 2 * odd

    def state_copy(t):
        return pltpu.make_async_remote_copy(
            src_ref=state_s.at[t],
            dst_ref=odd_state_s.at[t],
            send_sem=state_send.at[t],
            recv_sem=state_recv.at[t],
            device_id={"ctx": partner},
            device_id_type=MESH,
        )

    def suffix_copy(t):
        return pltpu.make_async_remote_copy(
            src_ref=odd_suffix_s.at[t],
            dst_ref=suffix_in_s.at[t],
            send_sem=suffix_send.at[t],
            recv_sem=suffix_recv.at[t],
            device_id={"ctx": partner},
            device_id_type=MESH,
        )

    def pair_copy(d, t):
        return pltpu.make_async_remote_copy(
            src_ref=pair_s.at[t],
            dst_ref=pair_in_s.at[d - 1, t],
            send_sem=pair_send.at[d - 1, t],
            recv_sem=pair_recv.at[d - 1, t],
            device_id={"ctx": lax.rem(me - 2 * d + 1 + ctx_count, ctx_count)},
            device_id_type=MESH,
        )

    for t in range(IN_FLIGHT):
        grad_copy(t).start()

    @pl.loop(0, chunks)
    def _(t):
        for i in range(3):
            load_copy(i, t).start()

    prefix_copy = pltpu.make_async_copy(prefix_hbm.at[0, 0], prefix_s, prefix_sem)
    prefix_copy.start()

    rows = lax.broadcasted_iota(jnp.int32, (length, length), 0)
    cols = lax.broadcasted_iota(jnp.int32, (length, length), 1)
    ordered = rows <= cols
    running = dot(
        decay_ref[0], jnp.where(ordered, 1.0, 0.0), 1, 0, precision=lax.Precision.HIGHEST
    )
    run_s[...] = running
    doc_row = doc_ref[...].astype(jnp.float32)
    first_doc = jnp.broadcast_to(doc_row[:, 0:1], (8, LANES))
    last_doc = jnp.broadcast_to(doc_row[:, length - 1 : length], (8, LANES))
    meta_own[0:heads] = jnp.broadcast_to(
        jnp.exp(running[:, length - 1 : length]), (heads, LANES)
    )
    meta_own[heads : heads + 8] = first_doc
    meta_own[heads + 8 : heads + 16] = last_doc
    meta_all[me] = meta_own[...]
    for k in range(1, ctx_count):
        meta_copy(k).start()

    doc_cols = as_columns(doc_row, LANES)
    doc_wide = jnp.concatenate([doc_cols] * blocks, axis=1)
    bias_s[...] = jnp.where(ordered & (doc_wide == doc_row), 0.0, MASKED)
    tail_mask_s[...] = jnp.where(doc_cols == last_doc[0:1], 1.0, 0.0)

    @pl.loop(0, heads)
    def _(h):
        col_s[h] = as_columns(run_s[pl.ds(h, 1), :], LANES)

    for k in range(1, ctx_count):
        meta_arrival(k).wait_recv()
    for b in range(ctx_count):
        first_here = meta_all[b, heads : heads + 8]
        last_here = meta_all[b, heads + 8 : heads + 16]
        if b > 0:
            last_before = meta_all[b - 1, heads + 8 : heads + 16]
            continues = jnp.where(first_here == last_before, 1.0, 0.0)
        else:
            continues = jnp.zeros((8, LANES), jnp.float32)
        cont_s[b] = continues
        passes = jnp.where(first_here == last_here, continues, 0.0)
        link_s[b] = meta_all[b, 0:heads] * passes[0:1]
    head_mask_s[...] = jnp.where(doc_cols == first_doc[0:1], 1.0, 0.0) * cont_s[me][0:1]
    prefix_copy.wait()

    def part(u):
        return slice(u * head_dim, (u + 1) * head_dim)

    def head_weight(h):
        return jnp.exp(col_s[h]) * head_mask_s[...]

    def stage_state(t):
        grad_copy(t).wait_recv()
        load_copy(0, t).wait()
        for u in range(CHUNK_HEADS):
            weighted = head_weight(t * CHUNK_HEADS + u) * g_s[t, :, part(u)].astype(jnp.float32)
            state_s[t, u] = dot(q_s[t, :, part(u)], weighted.astype(jnp.bfloat16), 0, 0)

        @pl.when(odd == 1)
        def _():
            state_copy(t).start()

        grad_copy(t).wait_send()

        @pl.when(t + IN_FLIGHT < chunks)
        def _():
            grad_copy(t + IN_FLIGHT).start()

    def stage_pair(t):
        state_copy(t).wait_recv()
        for u in range(CHUNK_HEADS):
            link = link_s[me, pl.ds(t * CHUNK_HEADS + u, 1), :]
            pair_s[t, u] = state_s[t, u] + link * odd_state_s[t, u]
        for d in range(1, reach + 1):

            @pl.when(pair >= d)
            def _():
                pair_copy(d, t).start()

    def stage_suffix(t):
        odd_suffix_s[t] = jnp.zeros(odd_suffix_s.shape[1:], jnp.float32)
        for d in range(1, reach + 1):

            @pl.when(pair + d < pairs)
            def _():
                pair_copy(d, t).wait_recv()
                for u in range(CHUNK_HEADS):
                    term = pair_in_s[d - 1, t, u]
                    for b in range(1, 2 * d - 1):
                        term = term * link_s[me + b, pl.ds(t * CHUNK_HEADS + u, 1), :]
                    odd_suffix_s[t, u] += term

        suffix_copy(t).start()

    def stage_inner(t, u):
        h = t * CHUNK_HEADS + u
        slot = lax.rem(t, SLOTS)
        q, k, v, g = (ref[t, :, part(u)] for ref in (q_s, k_s, v_s, g_s))
        row = run_s[pl.ds(h, 1), :]
        grad_q = [None] * blocks
        for block in range(blocks):
            low, high = block * LANES, (block + 1) * LANES
            wide = jnp.concatenate([col_s[h, low:high, :]] * (blocks - block), axis=1)
            weight = jnp.exp((row[:, low:] - wide) + bias_s[low:high, low:])
            scores = dot(k[low:high], q[low:], 1, 1)
            grad_dots = dot(v[low:high], g[low:], 1, 1)
            attention = (weight * scores).astype(jnp.bfloat16)
            grad_mix = (weight * grad_dots).astype(jnp.bfloat16)
            inner_s[slot, 0, low:high, part(u)] = dot(grad_mix, q[low:], 1, 0)
            inner_s[slot, 1, low:high, part(u)] = dot(attention, g[low:], 1, 0)
            spread = dot(grad_mix, k[low:high], 0, 0)
            for i in range(block, blocks):
                piece = spread[(i - block) * LANES : (i - block + 1) * LANES]
                grad_q[i] = piece if grad_q[i] is None else grad_q[i] + piece
        prefix = prefix_s[h].astype(jnp.bfloat16)
        grad_q = jnp.concatenate(grad_q, axis=0) + dot(g, prefix, 1, 1) * head_weight(h)
        out_q[t, :, part(u)] = grad_q.astype(jnp.bfloat16)

    def stage_finish(t):
        slot = lax.rem(t, SLOTS)

        @pl.when(odd == 0)
        def _():
            suffix_copy(t).wait_recv()
            for u in range(CHUNK_HEADS):
                link = link_s[me + 1, pl.ds(t * CHUNK_HEADS + u, 1), :]
                odd_suffix_s[t, u] = odd_state_s[t, u] + link * suffix_in_s[t, u]

        for u in range(CHUNK_HEADS):
            h = t * CHUNK_HEADS + u
            suffix = odd_suffix_s[t, u].astype(jnp.bfloat16)
            tail = jnp.exp(col_s[h, length - 1 : length, :] - col_s[h]) * tail_mask_s[...]
            grad_k = inner_s[slot, 0, :, part(u)] + dot(v_s[t, :, part(u)], suffix, 1, 1) * tail
            grad_v = inner_s[slot, 1, :, part(u)] + dot(k_s[t, :, part(u)], suffix, 1, 0) * tail
            out_k[t, :, part(u)] = grad_k.astype(jnp.bfloat16)
            out_v[t, :, part(u)] = grad_v.astype(jnp.bfloat16)

    @pl.loop(0, chunks + 2)
    def _(step):
        @pl.when(step < chunks)
        def _():
            stage_state(step)
            load_copy(1, step).wait()
            load_copy(2, step).wait()
            for u in range(CHUNK_HEADS - 1):
                stage_inner(step, u)

        @pl.when((step < chunks) & (odd == 0))
        def _():
            stage_pair(step)

        @pl.when(step < chunks)
        def _():
            stage_inner(step, CHUNK_HEADS - 1)

        @pl.when((step >= 1) & (step < chunks + 1) & (odd == 1))
        def _():
            stage_suffix(step - 1)

        @pl.when(step >= 2)
        def _():
            stage_finish(step - 2)

    for k in range(1, ctx_count):
        meta_copy(k).wait_send()

    @pl.loop(0, chunks)
    def _(t):
        @pl.when(odd == 1)
        def _():
            state_copy(t).wait_send()
            suffix_copy(t).wait_send()

        for d in range(1, reach + 1):

            @pl.when((odd == 0) & (pair >= d))
            def _():
                pair_copy(d, t).wait_send()


def place_kernel(in_q, in_k, in_v, out_q, out_k, out_v, sem):
    chunks, _, chunk_cols = in_q.shape
    copies = [
        pltpu.make_async_copy(
            source.at[t], target.at[0, :, t * chunk_cols : (t + 1) * chunk_cols], sem.at[i, t]
        )
        for i, (source, target) in enumerate(((in_q, out_q), (in_k, out_k), (in_v, out_v)))
        for t in range(chunks)
    ]
    for copy in copies:
        copy.start()
    for copy in copies:
        copy.wait()


def solution(mesh):
    pipe_count, ctx_count = mesh.shape["pipe"], mesh.shape["ctx"]

    def on_device(queries, key_rows, value_rows, next_grads, log_decay, doc_ids, prefix_states):
        _, length, width = queries.shape
        heads = log_decay.shape[1]
        head_dim = width // heads
        chunks = heads // CHUNK_HEADS
        chunk_cols = head_dim * CHUNK_HEADS
        reach = ctx_count // 4
        any_spec = pl.BlockSpec(memory_space=pl.ANY)
        vmem_spec = pl.BlockSpec(memory_space=pltpu.VMEM)
        f32, bf16 = jnp.float32, jnp.bfloat16
        rows = pltpu.VMEM((chunks, length, chunk_cols), bf16)
        states = pltpu.VMEM((chunks, CHUNK_HEADS, head_dim, head_dim), f32)
        mask = pltpu.VMEM((length, LANES), f32)
        dma = pltpu.SemaphoreType.DMA
        grads = pl.pallas_call(
            functools.partial(kernel, pipe_count, ctx_count),
            out_shape=[pltpu.VMEM((chunks, length, chunk_cols), bf16)] * 3,
            in_specs=[any_spec] * 4 + [vmem_spec] * 2 + [any_spec],
            out_specs=[vmem_spec] * 3,
            scratch_shapes=[
                rows,
                rows,
                rows,
                rows,
                pltpu.VMEM((heads, head_dim, head_dim), f32),
                pltpu.VMEM((heads, length), f32),
                pltpu.VMEM((heads, length, LANES), f32),
                pltpu.VMEM((length, length), f32),
                mask,
                mask,
                pltpu.VMEM((heads + 16, LANES), f32),
                pltpu.VMEM((ctx_count, heads + 16, LANES), f32),
                pltpu.VMEM((ctx_count, heads, LANES), f32),
                pltpu.VMEM((ctx_count, 8, LANES), f32),
                states,
                states,
                states,
                pltpu.VMEM((reach, chunks, CHUNK_HEADS, head_dim, head_dim), f32),
                states,
                states,
                pltpu.VMEM((SLOTS, 2, length, chunk_cols), f32),
                dma((3, chunks)),
                dma,
                dma((chunks,)),
                dma((chunks,)),
                dma((ctx_count,)),
                dma((ctx_count,)),
                dma((chunks,)),
                dma((chunks,)),
                dma((reach, chunks)),
                dma((reach, chunks)),
                dma((chunks,)),
                dma((chunks,)),
            ],
            compiler_params=pltpu.CompilerParams(
                collective_id=0, has_side_effects=True, vmem_limit_bytes=50 * 1024 * 1024
            ),
        )(queries, key_rows, value_rows, next_grads, log_decay, doc_ids, prefix_states)
        return pl.pallas_call(
            place_kernel,
            out_shape=[jax.ShapeDtypeStruct(queries.shape, bf16)] * 3,
            in_specs=[vmem_spec] * 3,
            out_specs=[any_spec] * 3,
            scratch_shapes=[dma((3, chunks))],
            compiler_params=pltpu.CompilerParams(vmem_limit_bytes=12 * 1024 * 1024),
        )(*grads)

    return jax.shard_map(
        on_device,
        mesh=mesh,
        in_specs=(
            P("pipe", "ctx", None),
            P("pipe", "ctx", None),
            P("pipe", "ctx", None),
            P("pipe", "ctx", None),
            P("pipe", None, "ctx"),
            P("pipe", "ctx"),
            P("pipe", "ctx", None, None, None),
        ),
        out_specs=(P("pipe", "ctx", None), P("pipe", "ctx", None), P("pipe", "ctx", None)),
        check_vma=False,
    )
```

```python
import functools

import jax
import jax.numpy as jnp
from jax import lax
from jax.experimental import pallas as pl
from jax.experimental.pallas import tpu as pltpu
from jax.sharding import PartitionSpec as P

MESH = pl.DeviceIdType.MESH
LANES = 128
CHUNK_HEADS = 1
IN_FLIGHT = 4
SLOTS = 3
PLACE_PARTS = 8
MASKED = -1e30


def dot(a, b, a_dim, b_dim, precision=None):
    return lax.dot_general(
        a,
        b,
        (((a_dim,), (b_dim,)), ((), ())),
        precision=precision,
        preferred_element_type=jnp.float32,
    )


def as_columns(row, width):
    return jnp.broadcast_to(row, (width, row.shape[1])).T


def kernel(
    pipe_count,
    ctx_count,
    q_hbm,
    k_hbm,
    v_hbm,
    g_hbm,
    decay_hbm,
    doc_hbm,
    prefix_hbm,
    out_q,
    out_k,
    out_v,
    q_s,
    k_s,
    v_s,
    g_s,
    prefix_s,
    run_s,
    col_s,
    bias_s,
    head_mask_s,
    tail_mask_s,
    meta_own,
    meta_all,
    link_s,
    cont_s,
    decay_s,
    doc_s,
    total_s,
    state_s,
    odd_state_s,
    pair_s,
    pair_in_s,
    suffix_s,
    suffix_in_s,
    inner_s,
    load_sem,
    prefix_sem,
    small_sem,
    g_send,
    g_recv,
    meta_send,
    meta_recv,
    state_send,
    state_recv,
    pair_send,
    pair_recv,
    suffix_send,
    suffix_recv,
):
    chunks, length, chunk_cols = q_s.shape
    head_dim = chunk_cols // CHUNK_HEADS
    heads = run_s.shape[0]
    blocks = length // LANES
    pairs = ctx_count // 2
    reach = ctx_count // 4
    section = lax.axis_index("pipe")
    me = lax.axis_index("ctx")
    odd = lax.rem(me, 2)
    pair = me // 2
    earlier = lax.rem(section + pipe_count - 1, pipe_count)
    later = lax.rem(section + 1, pipe_count)

    barrier = pltpu.get_barrier_semaphore()
    pl.semaphore_signal(barrier, inc=1, device_id={"pipe": earlier}, device_id_type=MESH)
    pl.semaphore_signal(barrier, inc=1, device_id={"pipe": later}, device_id_type=MESH)
    for k in range(1, ctx_count):
        pl.semaphore_signal(
            barrier, inc=1, device_id={"ctx": lax.rem(me + k, ctx_count)}, device_id_type=MESH
        )
    pl.semaphore_wait(barrier, ctx_count + 1)

    def columns(t):
        return pl.ds(pl.multiple_of(t * chunk_cols, chunk_cols), chunk_cols)

    def grad_copy(t):
        return pltpu.make_async_remote_copy(
            src_ref=g_hbm.at[0, :, columns(t)],
            dst_ref=g_s.at[t],
            send_sem=g_send.at[t],
            recv_sem=g_recv.at[t],
            device_id={"pipe": earlier},
            device_id_type=MESH,
        )

    def load_copy(i, t):
        source, target = ((q_hbm, q_s), (k_hbm, k_s), (v_hbm, v_s))[i]
        return pltpu.make_async_copy(
            source.at[0, :, columns(t)], target.at[t], load_sem.at[i, t]
        )

    def meta_copy(k):
        return pltpu.make_async_remote_copy(
            src_ref=meta_own,
            dst_ref=meta_all.at[me],
            send_sem=meta_send.at[k],
            recv_sem=meta_recv.at[k],
            device_id={"ctx": lax.rem(me + k, ctx_count)},
            device_id_type=MESH,
        )

    def meta_arrival(k):
        return pltpu.make_async_remote_copy(
            src_ref=meta_own,
            dst_ref=meta_all.at[lax.rem(me + ctx_count - k, ctx_count)],
            send_sem=meta_send.at[k],
            recv_sem=meta_recv.at[k],
            device_id={"ctx": lax.rem(me + k, ctx_count)},
            device_id_type=MESH,
        )

    partner = me + 1 - 2 * odd

    def state_copy(t):
        return pltpu.make_async_remote_copy(
            src_ref=state_s.at[t],
            dst_ref=odd_state_s.at[t],
            send_sem=state_send.at[t],
            recv_sem=state_recv.at[t],
            device_id={"ctx": partner},
            device_id_type=MESH,
        )

    def suffix_copy(t):
        return pltpu.make_async_remote_copy(
            src_ref=suffix_s.at[t],
            dst_ref=suffix_in_s.at[t],
            send_sem=suffix_send.at[t],
            recv_sem=suffix_recv.at[t],
            device_id={"ctx": partner},
            device_id_type=MESH,
        )

    def pair_copy(d, t):
        return pltpu.make_async_remote_copy(
            src_ref=pair_s.at[t],
            dst_ref=pair_in_s.at[d - 1, t],
            send_sem=pair_send.at[d - 1, t],
            recv_sem=pair_recv.at[d - 1, t],
            device_id={"ctx": lax.rem(me - 2 * d + 1 + ctx_count, ctx_count)},
            device_id_type=MESH,
        )

    for t in range(IN_FLIGHT):
        grad_copy(t).start()
    decay_copy = pltpu.make_async_copy(decay_hbm.at[0], decay_s, small_sem.at[0])
    doc_copy = pltpu.make_async_copy(doc_hbm, doc_s, small_sem.at[1])
    decay_copy.start()
    doc_copy.start()

    @pl.loop(0, chunks)
    def _(t):
        for i in range(3):
            load_copy(i, t).start()

    prefix_copy = pltpu.make_async_copy(prefix_hbm.at[0, 0], prefix_s, prefix_sem)
    prefix_copy.start()

    rows = lax.broadcasted_iota(jnp.int32, (length, length), 0)
    cols = lax.broadcasted_iota(jnp.int32, (length, length), 1)
    ordered = rows <= cols
    decay_copy.wait()
    doc_copy.wait()
    running = dot(
        decay_s[...], jnp.where(ordered, 1.0, 0.0), 1, 0, precision=lax.Precision.HIGHEST
    )
    run_s[...] = running
    doc_row = doc_s[...].astype(jnp.float32)
    first_doc = jnp.broadcast_to(doc_row[:, 0:1], (8, LANES))
    last_doc = jnp.broadcast_to(doc_row[:, length - 1 : length], (8, LANES))
    meta_own[0:heads] = jnp.broadcast_to(
        jnp.exp(running[:, length - 1 : length]), (heads, LANES)
    )
    meta_own[heads : heads + 8] = first_doc
    meta_own[heads + 8 : heads + 16] = last_doc
    meta_all[me] = meta_own[...]
    for k in range(1, ctx_count):
        meta_copy(k).start()

    doc_cols = as_columns(doc_row, LANES)
    doc_wide = jnp.concatenate([doc_cols] * blocks, axis=1)
    bias_s[...] = jnp.where(ordered & (doc_wide == doc_row), 0.0, MASKED)
    tail_mask_s[...] = jnp.where(doc_cols == last_doc[0:1], 1.0, 0.0)

    @pl.loop(0, heads)
    def _(h):
        col_s[h] = as_columns(run_s[pl.ds(h, 1), :], LANES)

    for k in range(1, ctx_count):
        meta_arrival(k).wait_recv()
    for b in range(ctx_count):
        first_here = meta_all[b, heads : heads + 8]
        last_here = meta_all[b, heads + 8 : heads + 16]
        if b > 0:
            last_before = meta_all[b - 1, heads + 8 : heads + 16]
            continues = jnp.where(first_here == last_before, 1.0, 0.0)
        else:
            continues = jnp.zeros((8, LANES), jnp.float32)
        cont_s[b] = continues
        passes = jnp.where(first_here == last_here, continues, 0.0)
        link_s[b] = meta_all[b, 0:heads] * passes[0:1]
    head_mask_s[...] = jnp.where(doc_cols == first_doc[0:1], 1.0, 0.0) * cont_s[me][0:1]
    prefix_copy.wait()

    def head_columns(h):
        return pl.ds(pl.multiple_of(h * head_dim, head_dim), head_dim)

    def part(u):
        return slice(u * head_dim, (u + 1) * head_dim)

    def head_weight(h):
        return jnp.exp(col_s[h]) * head_mask_s[...]

    def stage_state(t):
        grad_copy(t).wait_recv()
        load_copy(0, t).wait()
        for u in range(CHUNK_HEADS):
            weighted = head_weight(t * CHUNK_HEADS + u) * g_s[t, :, part(u)].astype(jnp.float32)
            total_s[u] = dot(q_s[t, :, part(u)], weighted.astype(jnp.bfloat16), 0, 0)

        @pl.when(odd == 1)
        def _():
            state_s[t] = total_s[...].astype(jnp.bfloat16)
            state_copy(t).start()

        grad_copy(t).wait_send()

        @pl.when(t + IN_FLIGHT < chunks)
        def _():
            grad_copy(t + IN_FLIGHT).start()

    def stage_pair(t):
        state_copy(t).wait_recv()
        for u in range(CHUNK_HEADS):
            link = link_s[me, pl.ds(t * CHUNK_HEADS + u, 1), :]
            total = total_s[u] + link * odd_state_s[t, u].astype(jnp.float32)
            pair_s[t, u] = total.astype(jnp.bfloat16)
        for d in range(1, reach + 1):

            @pl.when(pair >= d)
            def _():
                pair_copy(d, t).start()

    def stage_suffix(t):
        total_s[...] = jnp.zeros(total_s.shape, jnp.float32)
        for d in range(1, reach + 1):

            @pl.when(pair + d < pairs)
            def _():
                pair_copy(d, t).wait_recv()
                for u in range(CHUNK_HEADS):
                    term = pair_in_s[d - 1, t, u].astype(jnp.float32)
                    for b in range(1, 2 * d - 1):
                        term = term * link_s[me + b, pl.ds(t * CHUNK_HEADS + u, 1), :]
                    total_s[u] += term

        suffix_s[t] = total_s[...].astype(jnp.bfloat16)
        suffix_copy(t).start()

    def stage_inner(t, u):
        h = t * CHUNK_HEADS + u
        slot = lax.rem(t, SLOTS)
        q, k, v, g = (ref[t, :, part(u)] for ref in (q_s, k_s, v_s, g_s))
        row = run_s[pl.ds(h, 1), :]
        grad_q = [None] * blocks
        for block in range(blocks):
            low, high = block * LANES, (block + 1) * LANES
            wide = jnp.concatenate([col_s[h, low:high, :]] * (blocks - block), axis=1)
            weight = jnp.exp((row[:, low:] - wide) + bias_s[low:high, low:])
            scores = dot(k[low:high], q[low:], 1, 1)
            grad_dots = dot(v[low:high], g[low:], 1, 1)
            attention = (weight * scores).astype(jnp.bfloat16)
            grad_mix = (weight * grad_dots).astype(jnp.bfloat16)
            inner_s[slot, 0, low:high, part(u)] = dot(grad_mix, q[low:], 1, 0)
            inner_s[slot, 1, low:high, part(u)] = dot(attention, g[low:], 1, 0)
            spread = dot(grad_mix, k[low:high], 0, 0)
            for i in range(block, blocks):
                piece = spread[(i - block) * LANES : (i - block + 1) * LANES]
                grad_q[i] = piece if grad_q[i] is None else grad_q[i] + piece
        prefix = prefix_s[h].astype(jnp.bfloat16)
        grad_q = jnp.concatenate(grad_q, axis=0) + dot(g, prefix, 1, 1) * head_weight(h)
        out_q[:, head_columns(h)] = grad_q.astype(jnp.bfloat16)

    def stage_finish(t):
        slot = lax.rem(t, SLOTS)

        @pl.when(odd == 0)
        def _():
            suffix_copy(t).wait_recv()
            for u in range(CHUNK_HEADS):
                link = link_s[me + 1, pl.ds(t * CHUNK_HEADS + u, 1), :]
                carried = link * suffix_in_s[t, u].astype(jnp.float32)
                total = odd_state_s[t, u].astype(jnp.float32) + carried
                suffix_s[t, u] = total.astype(jnp.bfloat16)

        for u in range(CHUNK_HEADS):
            h = t * CHUNK_HEADS + u
            suffix = suffix_s[t, u]
            tail = jnp.exp(col_s[h, length - 1 : length, :] - col_s[h]) * tail_mask_s[...]
            grad_k = inner_s[slot, 0, :, part(u)] + dot(v_s[t, :, part(u)], suffix, 1, 1) * tail
            grad_v = inner_s[slot, 1, :, part(u)] + dot(k_s[t, :, part(u)], suffix, 1, 0) * tail
            out_k[:, head_columns(h)] = grad_k.astype(jnp.bfloat16)
            out_v[:, head_columns(h)] = grad_v.astype(jnp.bfloat16)

    @pl.loop(0, chunks + 2)
    def _(step):
        @pl.when(step < chunks)
        def _():
            stage_state(step)
            load_copy(1, step).wait()
            load_copy(2, step).wait()
            stage_inner(step, 0)

        @pl.when((step < chunks) & (odd == 0))
        def _():
            stage_pair(step)

        @pl.when(step < chunks)
        def _():
            for u in range(1, CHUNK_HEADS):
                stage_inner(step, u)

        @pl.when((step >= 1) & (step < chunks + 1) & (odd == 1))
        def _():
            stage_suffix(step - 1)

        @pl.when(step >= 2)
        def _():
            stage_finish(step - 2)

    for k in range(1, ctx_count):
        meta_copy(k).wait_send()

    @pl.loop(0, chunks)
    def _(t):
        @pl.when(odd == 1)
        def _():
            state_copy(t).wait_send()
            suffix_copy(t).wait_send()

        for d in range(1, reach + 1):

            @pl.when((odd == 0) & (pair >= d))
            def _():
                pair_copy(d, t).wait_send()


def place_kernel(in_q, in_k, in_v, out_q, out_k, out_v, sem):
    rows = in_q.shape[0] // PLACE_PARTS
    copies = []
    for j in range(PLACE_PARTS):
        span = slice(j * rows, (j + 1) * rows)
        for i, (source, target) in enumerate(((in_q, out_q), (in_k, out_k), (in_v, out_v))):
            copies.append(
                pltpu.make_async_copy(source.at[span], target.at[0, span], sem.at[i, j])
            )
    for copy in copies:
        copy.start()
    for copy in copies:
        copy.wait()


def solution(mesh):
    pipe_count, ctx_count = mesh.shape["pipe"], mesh.shape["ctx"]

    def on_device(queries, key_rows, value_rows, next_grads, log_decay, doc_ids, prefix_states):
        _, length, width = queries.shape
        heads = log_decay.shape[1]
        head_dim = width // heads
        chunks = heads // CHUNK_HEADS
        chunk_cols = head_dim * CHUNK_HEADS
        reach = ctx_count // 4
        any_spec = pl.BlockSpec(memory_space=pl.ANY)
        vmem_spec = pl.BlockSpec(memory_space=pltpu.VMEM)
        f32, bf16 = jnp.float32, jnp.bfloat16
        rows = pltpu.VMEM((chunks, length, chunk_cols), bf16)
        states = pltpu.VMEM((chunks, CHUNK_HEADS, head_dim, head_dim), bf16)
        mask = pltpu.VMEM((length, LANES), f32)
        dma = pltpu.SemaphoreType.DMA
        grads = pl.pallas_call(
            functools.partial(kernel, pipe_count, ctx_count),
            out_shape=[pltpu.VMEM((length, width), bf16)] * 3,
            in_specs=[any_spec] * 7,
            out_specs=[vmem_spec] * 3,
            scratch_shapes=[
                rows,
                rows,
                rows,
                rows,
                pltpu.VMEM((heads, head_dim, head_dim), f32),
                pltpu.VMEM((heads, length), f32),
                pltpu.VMEM((heads, length, LANES), f32),
                pltpu.VMEM((length, length), f32),
                mask,
                mask,
                pltpu.VMEM((heads + 16, LANES), f32),
                pltpu.VMEM((ctx_count, heads + 16, LANES), f32),
                pltpu.VMEM((ctx_count, heads, LANES), f32),
                pltpu.VMEM((ctx_count, 8, LANES), f32),
                pltpu.VMEM((heads, length), f32),
                pltpu.VMEM((1, length), jnp.int32),
                pltpu.VMEM((CHUNK_HEADS, head_dim, head_dim), f32),
                states,
                states,
                states,
                pltpu.VMEM((reach, chunks, CHUNK_HEADS, head_dim, head_dim), bf16),
                states,
                states,
                pltpu.VMEM((SLOTS, 2, length, chunk_cols), f32),
                dma((3, chunks)),
                dma,
                dma((2,)),
                dma((chunks,)),
                dma((chunks,)),
                dma((ctx_count,)),
                dma((ctx_count,)),
                dma((chunks,)),
                dma((chunks,)),
                dma((reach, chunks)),
                dma((reach, chunks)),
                dma((chunks,)),
                dma((chunks,)),
            ],
            compiler_params=pltpu.CompilerParams(
                collective_id=0, has_side_effects=True, vmem_limit_bytes=46 * 1024 * 1024
            ),
        )(queries, key_rows, value_rows, next_grads, log_decay, doc_ids, prefix_states)
        return pl.pallas_call(
            place_kernel,
            out_shape=[jax.ShapeDtypeStruct(queries.shape, bf16)] * 3,
            in_specs=[vmem_spec] * 3,
            out_specs=[any_spec] * 3,
            scratch_shapes=[dma((3, PLACE_PARTS))],
            compiler_params=pltpu.CompilerParams(vmem_limit_bytes=12 * 1024 * 1024),
        )(*grads)

    return jax.shard_map(
        on_device,
        mesh=mesh,
        in_specs=(
            P("pipe", "ctx", None),
            P("pipe", "ctx", None),
            P("pipe", "ctx", None),
            P("pipe", "ctx", None),
            P("pipe", None, "ctx"),
            P("pipe", "ctx"),
            P("pipe", "ctx", None, None, None),
        ),
        out_specs=(P("pipe", "ctx", None), P("pipe", "ctx", None), P("pipe", "ctx", None)),
        check_vma=False,
    )
```

```python
import functools

import jax
import jax.numpy as jnp
from jax import lax
from jax.experimental import pallas as pl
from jax.experimental.pallas import tpu as pltpu
from jax.sharding import PartitionSpec as P

MESH = pl.DeviceIdType.MESH
LANES = 128
CHUNK_HEADS = 1
IN_FLIGHT = 4
PAIR_LAG = 1
SUFFIX_LAG = 3
FINISH_LAG = 5
SLOTS = FINISH_LAG + 1
PLACE_PARTS = 8
MASKED = -1e30


def dot(a, b, a_dim, b_dim, precision=None):
    return lax.dot_general(
        a,
        b,
        (((a_dim,), (b_dim,)), ((), ())),
        precision=precision,
        preferred_element_type=jnp.float32,
    )


def as_columns(row, width):
    return jnp.broadcast_to(row, (width, row.shape[1])).T


def kernel(
    pipe_count,
    ctx_count,
    q_hbm,
    k_hbm,
    v_hbm,
    g_hbm,
    decay_hbm,
    doc_hbm,
    prefix_hbm,
    out_q,
    out_k,
    out_v,
    q_s,
    k_s,
    v_s,
    g_s,
    prefix_s,
    run_s,
    col_s,
    bias_s,
    head_mask_s,
    tail_mask_s,
    meta_own,
    meta_all,
    link_s,
    cont_s,
    decay_s,
    doc_s,
    total_s,
    sum_s,
    state_s,
    odd_state_s,
    pair_s,
    pair_in_s,
    suffix_s,
    suffix_in_s,
    inner_s,
    load_sem,
    prefix_sem,
    small_sem,
    g_send,
    g_recv,
    meta_send,
    meta_recv,
    state_send,
    state_recv,
    pair_send,
    pair_recv,
    suffix_send,
    suffix_recv,
):
    chunks, length, chunk_cols = q_s.shape
    head_dim = chunk_cols // CHUNK_HEADS
    heads = run_s.shape[0]
    blocks = length // LANES
    pairs = ctx_count // 2
    reach = ctx_count // 4
    section = lax.axis_index("pipe")
    me = lax.axis_index("ctx")
    odd = lax.rem(me, 2)
    pair = me // 2
    earlier = lax.rem(section + pipe_count - 1, pipe_count)
    later = lax.rem(section + 1, pipe_count)

    barrier = pltpu.get_barrier_semaphore()
    pl.semaphore_signal(barrier, inc=1, device_id={"pipe": earlier}, device_id_type=MESH)
    pl.semaphore_signal(barrier, inc=1, device_id={"pipe": later}, device_id_type=MESH)
    for k in range(1, ctx_count):
        pl.semaphore_signal(
            barrier, inc=1, device_id={"ctx": lax.rem(me + k, ctx_count)}, device_id_type=MESH
        )
    pl.semaphore_wait(barrier, ctx_count + 1)

    def columns(t):
        return pl.ds(pl.multiple_of(t * chunk_cols, chunk_cols), chunk_cols)

    def grad_copy(t):
        return pltpu.make_async_remote_copy(
            src_ref=g_hbm.at[0, :, columns(t)],
            dst_ref=g_s.at[t],
            send_sem=g_send.at[t],
            recv_sem=g_recv.at[t],
            device_id={"pipe": earlier},
            device_id_type=MESH,
        )

    def load_copy(i, t):
        source, target = ((q_hbm, q_s), (k_hbm, k_s), (v_hbm, v_s))[i]
        return pltpu.make_async_copy(
            source.at[0, :, columns(t)], target.at[t], load_sem.at[i, t]
        )

    def meta_copy(k):
        return pltpu.make_async_remote_copy(
            src_ref=meta_own,
            dst_ref=meta_all.at[me],
            send_sem=meta_send.at[k],
            recv_sem=meta_recv.at[k],
            device_id={"ctx": lax.rem(me + k, ctx_count)},
            device_id_type=MESH,
        )

    def meta_arrival(k):
        return pltpu.make_async_remote_copy(
            src_ref=meta_own,
            dst_ref=meta_all.at[lax.rem(me + ctx_count - k, ctx_count)],
            send_sem=meta_send.at[k],
            recv_sem=meta_recv.at[k],
            device_id={"ctx": lax.rem(me + k, ctx_count)},
            device_id_type=MESH,
        )

    partner = me + 1 - 2 * odd

    def state_copy(t):
        return pltpu.make_async_remote_copy(
            src_ref=state_s.at[t],
            dst_ref=odd_state_s.at[t],
            send_sem=state_send.at[t],
            recv_sem=state_recv.at[t],
            device_id={"ctx": partner},
            device_id_type=MESH,
        )

    def suffix_copy(t):
        return pltpu.make_async_remote_copy(
            src_ref=suffix_s.at[t],
            dst_ref=suffix_in_s.at[t],
            send_sem=suffix_send.at[t],
            recv_sem=suffix_recv.at[t],
            device_id={"ctx": partner},
            device_id_type=MESH,
        )

    def pair_copy(d, t):
        return pltpu.make_async_remote_copy(
            src_ref=pair_s.at[t],
            dst_ref=pair_in_s.at[d - 1, t],
            send_sem=pair_send.at[d - 1, t],
            recv_sem=pair_recv.at[d - 1, t],
            device_id={"ctx": lax.rem(me - 2 * d + 1 + ctx_count, ctx_count)},
            device_id_type=MESH,
        )

    for t in range(IN_FLIGHT):
        grad_copy(t).start()
    decay_copy = pltpu.make_async_copy(decay_hbm.at[0], decay_s, small_sem.at[0])
    doc_copy = pltpu.make_async_copy(doc_hbm, doc_s, small_sem.at[1])
    decay_copy.start()
    doc_copy.start()

    @pl.loop(0, chunks)
    def _(t):
        for i in range(3):
            load_copy(i, t).start()

    prefix_copy = pltpu.make_async_copy(prefix_hbm.at[0, 0], prefix_s, prefix_sem)
    prefix_copy.start()

    rows = lax.broadcasted_iota(jnp.int32, (length, length), 0)
    cols = lax.broadcasted_iota(jnp.int32, (length, length), 1)
    ordered = rows <= cols
    decay_copy.wait()
    doc_copy.wait()
    running = dot(
        decay_s[...], jnp.where(ordered, 1.0, 0.0), 1, 0, precision=lax.Precision.HIGHEST
    )
    run_s[...] = running
    doc_row = doc_s[...].astype(jnp.float32)
    first_doc = jnp.broadcast_to(doc_row[:, 0:1], (8, LANES))
    last_doc = jnp.broadcast_to(doc_row[:, length - 1 : length], (8, LANES))
    meta_own[0:heads] = jnp.broadcast_to(
        jnp.exp(running[:, length - 1 : length]), (heads, LANES)
    )
    meta_own[heads : heads + 8] = first_doc
    meta_own[heads + 8 : heads + 16] = last_doc
    meta_all[me] = meta_own[...]
    for k in range(1, ctx_count):
        meta_copy(k).start()

    doc_cols = as_columns(doc_row, LANES)
    doc_wide = jnp.concatenate([doc_cols] * blocks, axis=1)
    bias_s[...] = jnp.where(ordered & (doc_wide == doc_row), 0.0, MASKED)
    tail_mask_s[...] = jnp.where(doc_cols == last_doc[0:1], 1.0, 0.0)

    @pl.loop(0, heads)
    def _(h):
        col_s[h] = as_columns(run_s[pl.ds(h, 1), :], LANES)

    for k in range(1, ctx_count):
        meta_arrival(k).wait_recv()
    for b in range(ctx_count):
        first_here = meta_all[b, heads : heads + 8]
        last_here = meta_all[b, heads + 8 : heads + 16]
        if b > 0:
            last_before = meta_all[b - 1, heads + 8 : heads + 16]
            continues = jnp.where(first_here == last_before, 1.0, 0.0)
        else:
            continues = jnp.zeros((8, LANES), jnp.float32)
        cont_s[b] = continues
        passes = jnp.where(first_here == last_here, continues, 0.0)
        link_s[b] = meta_all[b, 0:heads] * passes[0:1]
    head_mask_s[...] = jnp.where(doc_cols == first_doc[0:1], 1.0, 0.0) * cont_s[me][0:1]
    prefix_copy.wait()

    def head_columns(h):
        return pl.ds(pl.multiple_of(h * head_dim, head_dim), head_dim)

    def part(u):
        return slice(u * head_dim, (u + 1) * head_dim)

    def head_weight(h):
        return jnp.exp(col_s[h]) * head_mask_s[...]

    def stage_state(t):
        grad_copy(t).wait_recv()
        load_copy(0, t).wait()
        for u in range(CHUNK_HEADS):
            weighted = head_weight(t * CHUNK_HEADS + u) * g_s[t, :, part(u)].astype(jnp.float32)
            total_s[lax.rem(t, 2), u] = dot(q_s[t, :, part(u)], weighted.astype(jnp.bfloat16), 0, 0)

        @pl.when(odd == 1)
        def _():
            state_s[t] = total_s[lax.rem(t, 2)].astype(jnp.bfloat16)
            state_copy(t).start()

        grad_copy(t).wait_send()

        @pl.when(t + IN_FLIGHT < chunks)
        def _():
            grad_copy(t + IN_FLIGHT).start()

    def stage_pair(t):
        state_copy(t).wait_recv()
        for u in range(CHUNK_HEADS):
            link = link_s[me, pl.ds(t * CHUNK_HEADS + u, 1), :]
            total = total_s[lax.rem(t, 2), u] + link * odd_state_s[t, u].astype(jnp.float32)
            pair_s[t, u] = total.astype(jnp.bfloat16)
        for d in range(1, reach + 1):

            @pl.when(pair >= d)
            def _():
                pair_copy(d, t).start()

    def stage_suffix(t):
        sum_s[...] = jnp.zeros(sum_s.shape, jnp.float32)
        for d in range(1, reach + 1):

            @pl.when(pair + d < pairs)
            def _():
                pair_copy(d, t).wait_recv()
                for u in range(CHUNK_HEADS):
                    term = pair_in_s[d - 1, t, u].astype(jnp.float32)
                    for b in range(1, 2 * d - 1):
                        term = term * link_s[me + b, pl.ds(t * CHUNK_HEADS + u, 1), :]
                    sum_s[u] += term

        suffix_s[t] = sum_s[...].astype(jnp.bfloat16)
        suffix_copy(t).start()

    def stage_inner(t, u):
        h = t * CHUNK_HEADS + u
        slot = lax.rem(t, SLOTS)
        q, k, v, g = (ref[t, :, part(u)] for ref in (q_s, k_s, v_s, g_s))
        row = run_s[pl.ds(h, 1), :]
        grad_q = [None] * blocks
        for block in range(blocks):
            low, high = block * LANES, (block + 1) * LANES
            wide = jnp.concatenate([col_s[h, low:high, :]] * (blocks - block), axis=1)
            weight = jnp.exp((row[:, low:] - wide) + bias_s[low:high, low:])
            scores = dot(k[low:high], q[low:], 1, 1)
            grad_dots = dot(v[low:high], g[low:], 1, 1)
            attention = (weight * scores).astype(jnp.bfloat16)
            grad_mix = (weight * grad_dots).astype(jnp.bfloat16)
            inner_s[slot, 0, low:high, part(u)] = dot(grad_mix, q[low:], 1, 0)
            inner_s[slot, 1, low:high, part(u)] = dot(attention, g[low:], 1, 0)
            spread = dot(grad_mix, k[low:high], 0, 0)
            for i in range(block, blocks):
                piece = spread[(i - block) * LANES : (i - block + 1) * LANES]
                grad_q[i] = piece if grad_q[i] is None else grad_q[i] + piece
        prefix = prefix_s[h].astype(jnp.bfloat16)
        grad_q = jnp.concatenate(grad_q, axis=0) + dot(g, prefix, 1, 1) * head_weight(h)
        out_q[:, head_columns(h)] = grad_q.astype(jnp.bfloat16)

    def stage_finish(t):
        slot = lax.rem(t, SLOTS)

        @pl.when(odd == 0)
        def _():
            suffix_copy(t).wait_recv()
            for u in range(CHUNK_HEADS):
                link = link_s[me + 1, pl.ds(t * CHUNK_HEADS + u, 1), :]
                carried = link * suffix_in_s[t, u].astype(jnp.float32)
                total = odd_state_s[t, u].astype(jnp.float32) + carried
                suffix_s[t, u] = total.astype(jnp.bfloat16)

        for u in range(CHUNK_HEADS):
            h = t * CHUNK_HEADS + u
            suffix = suffix_s[t, u]
            tail = jnp.exp(col_s[h, length - 1 : length, :] - col_s[h]) * tail_mask_s[...]
            grad_k = inner_s[slot, 0, :, part(u)] + dot(v_s[t, :, part(u)], suffix, 1, 1) * tail
            grad_v = inner_s[slot, 1, :, part(u)] + dot(k_s[t, :, part(u)], suffix, 1, 0) * tail
            out_k[:, head_columns(h)] = grad_k.astype(jnp.bfloat16)
            out_v[:, head_columns(h)] = grad_v.astype(jnp.bfloat16)

    @pl.loop(0, chunks + FINISH_LAG)
    def _(step):
        @pl.when((step >= PAIR_LAG) & (step < chunks + PAIR_LAG) & (odd == 0))
        def _():
            stage_pair(step - PAIR_LAG)

        @pl.when((step >= SUFFIX_LAG) & (step < chunks + SUFFIX_LAG) & (odd == 1))
        def _():
            stage_suffix(step - SUFFIX_LAG)

        @pl.when(step < chunks)
        def _():
            stage_state(step)
            load_copy(1, step).wait()
            load_copy(2, step).wait()
            for u in range(CHUNK_HEADS):
                stage_inner(step, u)

        @pl.when(step >= FINISH_LAG)
        def _():
            stage_finish(step - FINISH_LAG)

    for k in range(1, ctx_count):
        meta_copy(k).wait_send()

    @pl.loop(0, chunks)
    def _(t):
        @pl.when(odd == 1)
        def _():
            state_copy(t).wait_send()
            suffix_copy(t).wait_send()

        for d in range(1, reach + 1):

            @pl.when((odd == 0) & (pair >= d))
            def _():
                pair_copy(d, t).wait_send()


def place_kernel(in_q, in_k, in_v, out_q, out_k, out_v, sem):
    rows = in_q.shape[0] // PLACE_PARTS
    copies = []
    for j in range(PLACE_PARTS):
        span = slice(j * rows, (j + 1) * rows)
        for i, (source, target) in enumerate(((in_q, out_q), (in_k, out_k), (in_v, out_v))):
            copies.append(
                pltpu.make_async_copy(source.at[span], target.at[0, span], sem.at[i, j])
            )
    for copy in copies:
        copy.start()
    for copy in copies:
        copy.wait()


def solution(mesh):
    pipe_count, ctx_count = mesh.shape["pipe"], mesh.shape["ctx"]

    def on_device(queries, key_rows, value_rows, next_grads, log_decay, doc_ids, prefix_states):
        _, length, width = queries.shape
        heads = log_decay.shape[1]
        head_dim = width // heads
        chunks = heads // CHUNK_HEADS
        chunk_cols = head_dim * CHUNK_HEADS
        reach = ctx_count // 4
        any_spec = pl.BlockSpec(memory_space=pl.ANY)
        vmem_spec = pl.BlockSpec(memory_space=pltpu.VMEM)
        f32, bf16 = jnp.float32, jnp.bfloat16
        rows = pltpu.VMEM((chunks, length, chunk_cols), bf16)
        states = pltpu.VMEM((chunks, CHUNK_HEADS, head_dim, head_dim), bf16)
        mask = pltpu.VMEM((length, LANES), f32)
        dma = pltpu.SemaphoreType.DMA
        grads = pl.pallas_call(
            functools.partial(kernel, pipe_count, ctx_count),
            out_shape=[pltpu.VMEM((length, width), bf16)] * 3,
            in_specs=[any_spec] * 7,
            out_specs=[vmem_spec] * 3,
            scratch_shapes=[
                rows,
                rows,
                rows,
                rows,
                pltpu.VMEM((heads, head_dim, head_dim), f32),
                pltpu.VMEM((heads, length), f32),
                pltpu.VMEM((heads, length, LANES), f32),
                pltpu.VMEM((length, length), f32),
                mask,
                mask,
                pltpu.VMEM((heads + 16, LANES), f32),
                pltpu.VMEM((ctx_count, heads + 16, LANES), f32),
                pltpu.VMEM((ctx_count, heads, LANES), f32),
                pltpu.VMEM((ctx_count, 8, LANES), f32),
                pltpu.VMEM((heads, length), f32),
                pltpu.VMEM((1, length), jnp.int32),
                pltpu.VMEM((2, CHUNK_HEADS, head_dim, head_dim), f32),
                pltpu.VMEM((CHUNK_HEADS, head_dim, head_dim), f32),
                states,
                states,
                states,
                pltpu.VMEM((reach, chunks, CHUNK_HEADS, head_dim, head_dim), bf16),
                states,
                states,
                pltpu.VMEM((SLOTS, 2, length, chunk_cols), f32),
                dma((3, chunks)),
                dma,
                dma((2,)),
                dma((chunks,)),
                dma((chunks,)),
                dma((ctx_count,)),
                dma((ctx_count,)),
                dma((chunks,)),
                dma((chunks,)),
                dma((reach, chunks)),
                dma((reach, chunks)),
                dma((chunks,)),
                dma((chunks,)),
            ],
            compiler_params=pltpu.CompilerParams(
                collective_id=0, has_side_effects=True, vmem_limit_bytes=46 * 1024 * 1024
            ),
        )(queries, key_rows, value_rows, next_grads, log_decay, doc_ids, prefix_states)
        return pl.pallas_call(
            place_kernel,
            out_shape=[jax.ShapeDtypeStruct(queries.shape, bf16)] * 3,
            in_specs=[vmem_spec] * 3,
            out_specs=[any_spec] * 3,
            scratch_shapes=[dma((3, PLACE_PARTS))],
            compiler_params=pltpu.CompilerParams(vmem_limit_bytes=12 * 1024 * 1024),
        )(*grads)

    return jax.shard_map(
        on_device,
        mesh=mesh,
        in_specs=(
            P("pipe", "ctx", None),
            P("pipe", "ctx", None),
            P("pipe", "ctx", None),
            P("pipe", "ctx", None),
            P("pipe", None, "ctx"),
            P("pipe", "ctx"),
            P("pipe", "ctx", None, None, None),
        ),
        out_specs=(P("pipe", "ctx", None), P("pipe", "ctx", None), P("pipe", "ctx", None)),
        check_vma=False,
    )
```

```python
import functools

import jax
import jax.numpy as jnp
from jax import lax
from jax.experimental import pallas as pl
from jax.experimental.pallas import tpu as pltpu
from jax.sharding import PartitionSpec as P

MESH = pl.DeviceIdType.MESH
LANES = 128
CHUNK_HEADS = 1
IN_FLIGHT = 4
PAIR_LAG = 1
SUFFIX_LAG = 3
FINISH_LAG = 4
SLOTS = FINISH_LAG + 1
PLACE_PARTS = 8
MASKED = -1e30


def dot(a, b, a_dim, b_dim, precision=None):
    return lax.dot_general(
        a,
        b,
        (((a_dim,), (b_dim,)), ((), ())),
        precision=precision,
        preferred_element_type=jnp.float32,
    )


def as_columns(row, width):
    return jnp.broadcast_to(row, (width, row.shape[1])).T


def kernel(
    pipe_count,
    ctx_count,
    q_hbm,
    k_hbm,
    v_hbm,
    g_hbm,
    decay_hbm,
    doc_hbm,
    prefix_hbm,
    out_q,
    out_k,
    out_v,
    q_s,
    k_s,
    v_s,
    g_s,
    g_own_s,
    prefix_s,
    run_s,
    col_s,
    bias_s,
    head_mask_s,
    tail_mask_s,
    meta_own,
    meta_all,
    link_s,
    cont_s,
    decay_s,
    doc_s,
    total_s,
    sum_s,
    state_s,
    odd_state_s,
    pair_s,
    pair_in_s,
    suffix_s,
    suffix_in_s,
    inner_s,
    load_sem,
    prefix_sem,
    small_sem,
    g_send,
    g_recv,
    meta_send,
    meta_recv,
    state_send,
    state_recv,
    pair_send,
    pair_recv,
    suffix_send,
    suffix_recv,
):
    chunks, length, chunk_cols = q_s.shape
    head_dim = chunk_cols // CHUNK_HEADS
    heads = run_s.shape[0]
    blocks = length // LANES
    pairs = ctx_count // 2
    reach = ctx_count // 4
    section = lax.axis_index("pipe")
    me = lax.axis_index("ctx")
    odd = lax.rem(me, 2)
    pair = me // 2
    earlier = lax.rem(section + pipe_count - 1, pipe_count)
    later = lax.rem(section + 1, pipe_count)

    def columns(t):
        return pl.ds(pl.multiple_of(t * chunk_cols, chunk_cols), chunk_cols)

    def grad_copy(t):
        return pltpu.make_async_remote_copy(
            src_ref=g_own_s.at[t],
            dst_ref=g_s.at[t],
            send_sem=g_send.at[t],
            recv_sem=g_recv.at[t],
            device_id={"pipe": earlier},
            device_id_type=MESH,
        )

    def load_copy(i, t):
        source, target = ((q_hbm, q_s), (k_hbm, k_s), (v_hbm, v_s), (g_hbm, g_own_s))[i]
        return pltpu.make_async_copy(
            source.at[0, :, columns(t)], target.at[t], load_sem.at[i, t]
        )

    def meta_copy(k):
        return pltpu.make_async_remote_copy(
            src_ref=meta_own,
            dst_ref=meta_all.at[me],
            send_sem=meta_send.at[k],
            recv_sem=meta_recv.at[k],
            device_id={"ctx": lax.rem(me + k, ctx_count)},
            device_id_type=MESH,
        )

    def meta_arrival(k):
        return pltpu.make_async_remote_copy(
            src_ref=meta_own,
            dst_ref=meta_all.at[lax.rem(me + ctx_count - k, ctx_count)],
            send_sem=meta_send.at[k],
            recv_sem=meta_recv.at[k],
            device_id={"ctx": lax.rem(me + k, ctx_count)},
            device_id_type=MESH,
        )

    partner = me + 1 - 2 * odd

    def state_copy(t):
        return pltpu.make_async_remote_copy(
            src_ref=state_s.at[t],
            dst_ref=odd_state_s.at[t],
            send_sem=state_send.at[t],
            recv_sem=state_recv.at[t],
            device_id={"ctx": partner},
            device_id_type=MESH,
        )

    def suffix_copy(t):
        return pltpu.make_async_remote_copy(
            src_ref=suffix_s.at[t],
            dst_ref=suffix_in_s.at[t],
            send_sem=suffix_send.at[t],
            recv_sem=suffix_recv.at[t],
            device_id={"ctx": partner},
            device_id_type=MESH,
        )

    def pair_copy(d, t):
        return pltpu.make_async_remote_copy(
            src_ref=pair_s.at[t],
            dst_ref=pair_in_s.at[d - 1, t],
            send_sem=pair_send.at[d - 1, t],
            recv_sem=pair_recv.at[d - 1, t],
            device_id={"ctx": lax.rem(me - 2 * d + 1 + ctx_count, ctx_count)},
            device_id_type=MESH,
        )

    @pl.loop(0, chunks)
    def _(t):
        load_copy(3, t).start()

    decay_copy = pltpu.make_async_copy(decay_hbm.at[0], decay_s, small_sem.at[0])
    doc_copy = pltpu.make_async_copy(doc_hbm, doc_s, small_sem.at[1])
    decay_copy.start()
    doc_copy.start()

    barrier = pltpu.get_barrier_semaphore()
    pl.semaphore_signal(barrier, inc=1, device_id={"pipe": earlier}, device_id_type=MESH)
    pl.semaphore_signal(barrier, inc=1, device_id={"pipe": later}, device_id_type=MESH)
    for k in range(1, ctx_count):
        pl.semaphore_signal(
            barrier, inc=1, device_id={"ctx": lax.rem(me + k, ctx_count)}, device_id_type=MESH
        )
    pl.semaphore_wait(barrier, ctx_count + 1)

    for t in range(IN_FLIGHT):
        load_copy(3, t).wait()
        grad_copy(t).start()

    @pl.loop(0, chunks)
    def _(t):
        for i in range(3):
            load_copy(i, t).start()

    prefix_copy = pltpu.make_async_copy(prefix_hbm.at[0, 0], prefix_s, prefix_sem)
    prefix_copy.start()

    rows = lax.broadcasted_iota(jnp.int32, (length, length), 0)
    cols = lax.broadcasted_iota(jnp.int32, (length, length), 1)
    ordered = rows <= cols
    decay_copy.wait()
    doc_copy.wait()
    running = dot(
        decay_s[...], jnp.where(ordered, 1.0, 0.0), 1, 0, precision=lax.Precision.HIGHEST
    )
    run_s[...] = running
    doc_row = doc_s[...].astype(jnp.float32)
    first_doc = jnp.broadcast_to(doc_row[:, 0:1], (8, LANES))
    last_doc = jnp.broadcast_to(doc_row[:, length - 1 : length], (8, LANES))
    meta_own[0:heads] = jnp.broadcast_to(
        jnp.exp(running[:, length - 1 : length]), (heads, LANES)
    )
    meta_own[heads : heads + 8] = first_doc
    meta_own[heads + 8 : heads + 16] = last_doc
    meta_all[me] = meta_own[...]
    for k in range(1, ctx_count):
        meta_copy(k).start()

    doc_cols = as_columns(doc_row, LANES)
    doc_wide = jnp.concatenate([doc_cols] * blocks, axis=1)
    bias_s[...] = jnp.where(ordered & (doc_wide == doc_row), 0.0, MASKED)
    tail_mask_s[...] = jnp.where(doc_cols == last_doc[0:1], 1.0, 0.0)

    @pl.loop(0, heads)
    def _(h):
        col_s[h] = as_columns(run_s[pl.ds(h, 1), :], LANES)

    for k in range(1, ctx_count):
        meta_arrival(k).wait_recv()
    for b in range(ctx_count):
        first_here = meta_all[b, heads : heads + 8]
        last_here = meta_all[b, heads + 8 : heads + 16]
        if b > 0:
            last_before = meta_all[b - 1, heads + 8 : heads + 16]
            continues = jnp.where(first_here == last_before, 1.0, 0.0)
        else:
            continues = jnp.zeros((8, LANES), jnp.float32)
        cont_s[b] = continues
        passes = jnp.where(first_here == last_here, continues, 0.0)
        link_s[b] = meta_all[b, 0:heads] * passes[0:1]
    head_mask_s[...] = jnp.where(doc_cols == first_doc[0:1], 1.0, 0.0) * cont_s[me][0:1]
    prefix_copy.wait()

    def head_columns(h):
        return pl.ds(pl.multiple_of(h * head_dim, head_dim), head_dim)

    def part(u):
        return slice(u * head_dim, (u + 1) * head_dim)

    def head_weight(h):
        return jnp.exp(col_s[h]) * head_mask_s[...]

    def stage_state(t):
        grad_copy(t).wait_recv()
        grad_copy(t).wait_send()

        @pl.when(t + IN_FLIGHT < chunks)
        def _():
            load_copy(3, t + IN_FLIGHT).wait()
            grad_copy(t + IN_FLIGHT).start()

        load_copy(0, t).wait()
        for u in range(CHUNK_HEADS):
            weighted = head_weight(t * CHUNK_HEADS + u) * g_s[t, :, part(u)].astype(jnp.float32)
            total_s[lax.rem(t, 2), u] = dot(q_s[t, :, part(u)], weighted.astype(jnp.bfloat16), 0, 0)

        @pl.when(odd == 1)
        def _():
            state_s[t] = total_s[lax.rem(t, 2)].astype(jnp.bfloat16)
            state_copy(t).start()


    def stage_pair(t):
        state_copy(t).wait_recv()
        for u in range(CHUNK_HEADS):
            link = link_s[me, pl.ds(t * CHUNK_HEADS + u, 1), :]
            total = total_s[lax.rem(t, 2), u] + link * odd_state_s[t, u].astype(jnp.float32)
            pair_s[t, u] = total.astype(jnp.bfloat16)
        for d in range(1, reach + 1):

            @pl.when(pair >= d)
            def _():
                pair_copy(d, t).start()

    def stage_suffix(t):
        sum_s[...] = jnp.zeros(sum_s.shape, jnp.float32)
        for d in range(1, reach + 1):

            @pl.when(pair + d < pairs)
            def _():
                pair_copy(d, t).wait_recv()
                for u in range(CHUNK_HEADS):
                    term = pair_in_s[d - 1, t, u].astype(jnp.float32)
                    for b in range(1, 2 * d - 1):
                        term = term * link_s[me + b, pl.ds(t * CHUNK_HEADS + u, 1), :]
                    sum_s[u] += term

        suffix_s[t] = sum_s[...].astype(jnp.bfloat16)
        suffix_copy(t).start()

    def stage_inner(t, u):
        h = t * CHUNK_HEADS + u
        slot = lax.rem(t, SLOTS)
        q, k, v, g = (ref[t, :, part(u)] for ref in (q_s, k_s, v_s, g_s))
        row = run_s[pl.ds(h, 1), :]
        grad_q = [None] * blocks
        for block in range(blocks):
            low, high = block * LANES, (block + 1) * LANES
            wide = jnp.concatenate([col_s[h, low:high, :]] * (blocks - block), axis=1)
            weight = jnp.exp((row[:, low:] - wide) + bias_s[low:high, low:])
            scores = dot(k[low:high], q[low:], 1, 1)
            grad_dots = dot(v[low:high], g[low:], 1, 1)
            attention = (weight * scores).astype(jnp.bfloat16)
            grad_mix = (weight * grad_dots).astype(jnp.bfloat16)
            inner_s[slot, 0, low:high, part(u)] = dot(grad_mix, q[low:], 1, 0)
            inner_s[slot, 1, low:high, part(u)] = dot(attention, g[low:], 1, 0)
            spread = dot(grad_mix, k[low:high], 0, 0)
            for i in range(block, blocks):
                piece = spread[(i - block) * LANES : (i - block + 1) * LANES]
                grad_q[i] = piece if grad_q[i] is None else grad_q[i] + piece
        prefix = prefix_s[h].astype(jnp.bfloat16)
        grad_q = jnp.concatenate(grad_q, axis=0) + dot(g, prefix, 1, 1) * head_weight(h)
        out_q[:, head_columns(h)] = grad_q.astype(jnp.bfloat16)

    def stage_finish(t):
        slot = lax.rem(t, SLOTS)

        @pl.when(odd == 0)
        def _():
            suffix_copy(t).wait_recv()
            for u in range(CHUNK_HEADS):
                link = link_s[me + 1, pl.ds(t * CHUNK_HEADS + u, 1), :]
                carried = link * suffix_in_s[t, u].astype(jnp.float32)
                total = odd_state_s[t, u].astype(jnp.float32) + carried
                suffix_s[t, u] = total.astype(jnp.bfloat16)

        for u in range(CHUNK_HEADS):
            h = t * CHUNK_HEADS + u
            suffix = suffix_s[t, u]
            tail = jnp.exp(col_s[h, length - 1 : length, :] - col_s[h]) * tail_mask_s[...]
            grad_k = inner_s[slot, 0, :, part(u)] + dot(v_s[t, :, part(u)], suffix, 1, 1) * tail
            grad_v = inner_s[slot, 1, :, part(u)] + dot(k_s[t, :, part(u)], suffix, 1, 0) * tail
            out_k[:, head_columns(h)] = grad_k.astype(jnp.bfloat16)
            out_v[:, head_columns(h)] = grad_v.astype(jnp.bfloat16)

    @pl.loop(0, chunks + FINISH_LAG)
    def _(step):
        @pl.when((step >= PAIR_LAG) & (step < chunks + PAIR_LAG) & (odd == 0))
        def _():
            stage_pair(step - PAIR_LAG)

        @pl.when((step >= SUFFIX_LAG) & (step < chunks + SUFFIX_LAG) & (odd == 1))
        def _():
            stage_suffix(step - SUFFIX_LAG)

        @pl.when(step < chunks)
        def _():
            stage_state(step)
            load_copy(1, step).wait()
            load_copy(2, step).wait()
            for u in range(CHUNK_HEADS):
                stage_inner(step, u)

        @pl.when(step >= FINISH_LAG)
        def _():
            stage_finish(step - FINISH_LAG)

    for k in range(1, ctx_count):
        meta_copy(k).wait_send()

    @pl.loop(0, chunks)
    def _(t):
        @pl.when(odd == 1)
        def _():
            state_copy(t).wait_send()
            suffix_copy(t).wait_send()

        for d in range(1, reach + 1):

            @pl.when((odd == 0) & (pair >= d))
            def _():
                pair_copy(d, t).wait_send()


def place_kernel(in_q, in_k, in_v, out_q, out_k, out_v, sem):
    rows = in_q.shape[0] // PLACE_PARTS
    copies = []
    for j in range(PLACE_PARTS):
        span = slice(j * rows, (j + 1) * rows)
        for i, (source, target) in enumerate(((in_q, out_q), (in_k, out_k), (in_v, out_v))):
            copies.append(
                pltpu.make_async_copy(source.at[span], target.at[0, span], sem.at[i, j])
            )
    for copy in copies:
        copy.start()
    for copy in copies:
        copy.wait()


def solution(mesh):
    pipe_count, ctx_count = mesh.shape["pipe"], mesh.shape["ctx"]

    def on_device(queries, key_rows, value_rows, next_grads, log_decay, doc_ids, prefix_states):
        _, length, width = queries.shape
        heads = log_decay.shape[1]
        head_dim = width // heads
        chunks = heads // CHUNK_HEADS
        chunk_cols = head_dim * CHUNK_HEADS
        reach = ctx_count // 4
        any_spec = pl.BlockSpec(memory_space=pl.ANY)
        vmem_spec = pl.BlockSpec(memory_space=pltpu.VMEM)
        f32, bf16 = jnp.float32, jnp.bfloat16
        rows = pltpu.VMEM((chunks, length, chunk_cols), bf16)
        states = pltpu.VMEM((chunks, CHUNK_HEADS, head_dim, head_dim), bf16)
        mask = pltpu.VMEM((length, LANES), f32)
        dma = pltpu.SemaphoreType.DMA
        grads = pl.pallas_call(
            functools.partial(kernel, pipe_count, ctx_count),
            out_shape=[pltpu.VMEM((length, width), bf16)] * 3,
            in_specs=[any_spec] * 7,
            out_specs=[vmem_spec] * 3,
            scratch_shapes=[
                rows,
                rows,
                rows,
                rows,
                rows,
                pltpu.VMEM((heads, head_dim, head_dim), f32),
                pltpu.VMEM((heads, length), f32),
                pltpu.VMEM((heads, length, LANES), f32),
                pltpu.VMEM((length, length), f32),
                mask,
                mask,
                pltpu.VMEM((heads + 16, LANES), f32),
                pltpu.VMEM((ctx_count, heads + 16, LANES), f32),
                pltpu.VMEM((ctx_count, heads, LANES), f32),
                pltpu.VMEM((ctx_count, 8, LANES), f32),
                pltpu.VMEM((heads, length), f32),
                pltpu.VMEM((1, length), jnp.int32),
                pltpu.VMEM((2, CHUNK_HEADS, head_dim, head_dim), f32),
                pltpu.VMEM((CHUNK_HEADS, head_dim, head_dim), f32),
                states,
                states,
                states,
                pltpu.VMEM((reach, chunks, CHUNK_HEADS, head_dim, head_dim), bf16),
                states,
                states,
                pltpu.VMEM((SLOTS, 2, length, chunk_cols), f32),
                dma((4, chunks)),
                dma,
                dma((2,)),
                dma((chunks,)),
                dma((chunks,)),
                dma((ctx_count,)),
                dma((ctx_count,)),
                dma((chunks,)),
                dma((chunks,)),
                dma((reach, chunks)),
                dma((reach, chunks)),
                dma((chunks,)),
                dma((chunks,)),
            ],
            compiler_params=pltpu.CompilerParams(
                collective_id=0, has_side_effects=True, vmem_limit_bytes=46 * 1024 * 1024
            ),
        )(queries, key_rows, value_rows, next_grads, log_decay, doc_ids, prefix_states)
        return pl.pallas_call(
            place_kernel,
            out_shape=[jax.ShapeDtypeStruct(queries.shape, bf16)] * 3,
            in_specs=[vmem_spec] * 3,
            out_specs=[any_spec] * 3,
            scratch_shapes=[dma((3, PLACE_PARTS))],
            compiler_params=pltpu.CompilerParams(vmem_limit_bytes=12 * 1024 * 1024),
        )(*grads)

    return jax.shard_map(
        on_device,
        mesh=mesh,
        in_specs=(
            P("pipe", "ctx", None),
            P("pipe", "ctx", None),
            P("pipe", "ctx", None),
            P("pipe", "ctx", None),
            P("pipe", None, "ctx"),
            P("pipe", "ctx"),
            P("pipe", "ctx", None, None, None),
        ),
        out_specs=(P("pipe", "ctx", None), P("pipe", "ctx", None), P("pipe", "ctx", None)),
        check_vma=False,
    )
```

```python
import functools

import jax
import jax.numpy as jnp
from jax import lax
from jax.experimental import pallas as pl
from jax.experimental.pallas import tpu as pltpu
from jax.sharding import PartitionSpec as P

MESH = pl.DeviceIdType.MESH
LANES = 128
CHUNK_HEADS = 1
IN_FLIGHT = 4
SUFFIX_LAG = 3
FINISH_LAG = 4
SLOTS = FINISH_LAG + 1
PLACE_PARTS = 8
MASKED = -1e30


def dot(a, b, a_dim, b_dim, precision=None):
    return lax.dot_general(
        a,
        b,
        (((a_dim,), (b_dim,)), ((), ())),
        precision=precision,
        preferred_element_type=jnp.float32,
    )


def as_columns(row, width):
    return jnp.broadcast_to(row, (width, row.shape[1])).T


def kernel(
    pipe_count,
    ctx_count,
    q_hbm,
    k_hbm,
    v_hbm,
    g_hbm,
    decay_hbm,
    doc_hbm,
    prefix_hbm,
    out_q,
    out_k,
    out_v,
    q_s,
    k_s,
    v_s,
    g_s,
    prefix_s,
    run_s,
    col_s,
    bias_s,
    head_mask_s,
    tail_mask_s,
    meta_own,
    meta_all,
    link_s,
    cont_s,
    decay_s,
    doc_s,
    sum_s,
    state_s,
    odd_state_s,
    later_in_s,
    suffix_s,
    suffix_in_s,
    inner_s,
    load_sem,
    prefix_sem,
    small_sem,
    g_send,
    g_recv,
    meta_send,
    meta_recv,
    state_send,
    state_recv,
    later_send,
    later_recv,
    suffix_send,
    suffix_recv,
):
    chunks, length, chunk_cols = q_s.shape
    head_dim = chunk_cols // CHUNK_HEADS
    heads = run_s.shape[0]
    blocks = length // LANES
    pairs = ctx_count // 2
    reach = ctx_count // 4
    section = lax.axis_index("pipe")
    me = lax.axis_index("ctx")
    odd = lax.rem(me, 2)
    pair = me // 2
    earlier = lax.rem(section + pipe_count - 1, pipe_count)
    later = lax.rem(section + 1, pipe_count)

    barrier = pltpu.get_barrier_semaphore()
    pl.semaphore_signal(barrier, inc=1, device_id={"pipe": earlier}, device_id_type=MESH)
    pl.semaphore_signal(barrier, inc=1, device_id={"pipe": later}, device_id_type=MESH)
    for k in range(1, ctx_count):
        pl.semaphore_signal(
            barrier, inc=1, device_id={"ctx": lax.rem(me + k, ctx_count)}, device_id_type=MESH
        )
    pl.semaphore_wait(barrier, ctx_count + 1)

    def columns(t):
        return pl.ds(pl.multiple_of(t * chunk_cols, chunk_cols), chunk_cols)

    def grad_copy(t):
        return pltpu.make_async_remote_copy(
            src_ref=g_hbm.at[0, :, columns(t)],
            dst_ref=g_s.at[t],
            send_sem=g_send.at[t],
            recv_sem=g_recv.at[t],
            device_id={"pipe": earlier},
            device_id_type=MESH,
        )

    def load_copy(i, t):
        source, target = ((q_hbm, q_s), (k_hbm, k_s), (v_hbm, v_s))[i]
        return pltpu.make_async_copy(
            source.at[0, :, columns(t)], target.at[t], load_sem.at[i, t]
        )

    def meta_copy(k):
        return pltpu.make_async_remote_copy(
            src_ref=meta_own,
            dst_ref=meta_all.at[me],
            send_sem=meta_send.at[k],
            recv_sem=meta_recv.at[k],
            device_id={"ctx": lax.rem(me + k, ctx_count)},
            device_id_type=MESH,
        )

    def meta_arrival(k):
        return pltpu.make_async_remote_copy(
            src_ref=meta_own,
            dst_ref=meta_all.at[lax.rem(me + ctx_count - k, ctx_count)],
            send_sem=meta_send.at[k],
            recv_sem=meta_recv.at[k],
            device_id={"ctx": lax.rem(me + k, ctx_count)},
            device_id_type=MESH,
        )

    partner = me + 1 - 2 * odd

    def state_copy(t):
        return pltpu.make_async_remote_copy(
            src_ref=state_s.at[t],
            dst_ref=odd_state_s.at[t],
            send_sem=state_send.at[t],
            recv_sem=state_recv.at[t],
            device_id={"ctx": partner},
            device_id_type=MESH,
        )

    def suffix_copy(t):
        return pltpu.make_async_remote_copy(
            src_ref=suffix_s.at[t],
            dst_ref=suffix_in_s.at[t],
            send_sem=suffix_send.at[t],
            recv_sem=suffix_recv.at[t],
            device_id={"ctx": partner},
            device_id_type=MESH,
        )

    def later_copy(d, sender, t):
        return pltpu.make_async_remote_copy(
            src_ref=state_s.at[t],
            dst_ref=later_in_s.at[d - 1, sender, t],
            send_sem=later_send.at[d - 1, t],
            recv_sem=later_recv.at[d - 1, sender, t],
            device_id={"ctx": lax.rem(me - odd - 2 * d + 1 + ctx_count, ctx_count)},
            device_id_type=MESH,
        )

    for t in range(IN_FLIGHT):
        grad_copy(t).start()
    decay_copy = pltpu.make_async_copy(decay_hbm.at[0], decay_s, small_sem.at[0])
    doc_copy = pltpu.make_async_copy(doc_hbm, doc_s, small_sem.at[1])
    decay_copy.start()
    doc_copy.start()

    @pl.loop(0, chunks)
    def _(t):
        for i in range(3):
            load_copy(i, t).start()

    prefix_copy = pltpu.make_async_copy(prefix_hbm.at[0, 0], prefix_s, prefix_sem)
    prefix_copy.start()

    rows = lax.broadcasted_iota(jnp.int32, (length, length), 0)
    cols = lax.broadcasted_iota(jnp.int32, (length, length), 1)
    ordered = rows <= cols
    decay_copy.wait()
    doc_copy.wait()
    running = dot(
        decay_s[...], jnp.where(ordered, 1.0, 0.0), 1, 0, precision=lax.Precision.HIGHEST
    )
    run_s[...] = running
    doc_row = doc_s[...].astype(jnp.float32)
    first_doc = jnp.broadcast_to(doc_row[:, 0:1], (8, LANES))
    last_doc = jnp.broadcast_to(doc_row[:, length - 1 : length], (8, LANES))
    meta_own[0:heads] = jnp.broadcast_to(
        jnp.exp(running[:, length - 1 : length]), (heads, LANES)
    )
    meta_own[heads : heads + 8] = first_doc
    meta_own[heads + 8 : heads + 16] = last_doc
    meta_all[me] = meta_own[...]
    for k in range(1, ctx_count):
        meta_copy(k).start()

    doc_cols = as_columns(doc_row, LANES)
    doc_wide = jnp.concatenate([doc_cols] * blocks, axis=1)
    bias_s[...] = jnp.where(ordered & (doc_wide == doc_row), 0.0, MASKED)
    tail_mask_s[...] = jnp.where(doc_cols == last_doc[0:1], 1.0, 0.0)

    @pl.loop(0, heads)
    def _(h):
        col_s[h] = as_columns(run_s[pl.ds(h, 1), :], LANES)

    for k in range(1, ctx_count):
        meta_arrival(k).wait_recv()
    for b in range(ctx_count):
        first_here = meta_all[b, heads : heads + 8]
        last_here = meta_all[b, heads + 8 : heads + 16]
        if b > 0:
            last_before = meta_all[b - 1, heads + 8 : heads + 16]
            continues = jnp.where(first_here == last_before, 1.0, 0.0)
        else:
            continues = jnp.zeros((8, LANES), jnp.float32)
        cont_s[b] = continues
        passes = jnp.where(first_here == last_here, continues, 0.0)
        link_s[b] = meta_all[b, 0:heads] * passes[0:1]
    head_mask_s[...] = jnp.where(doc_cols == first_doc[0:1], 1.0, 0.0) * cont_s[me][0:1]
    prefix_copy.wait()

    def head_columns(h):
        return pl.ds(pl.multiple_of(h * head_dim, head_dim), head_dim)

    def part(u):
        return slice(u * head_dim, (u + 1) * head_dim)

    def head_weight(h):
        return jnp.exp(col_s[h]) * head_mask_s[...]

    def stage_state(t):
        grad_copy(t).wait_recv()
        load_copy(0, t).wait()
        for u in range(CHUNK_HEADS):
            weighted = head_weight(t * CHUNK_HEADS + u) * g_s[t, :, part(u)].astype(jnp.float32)
            state = dot(q_s[t, :, part(u)], weighted.astype(jnp.bfloat16), 0, 0)
            state_s[t, u] = state.astype(jnp.bfloat16)
        for d in range(1, reach + 1):

            @pl.when(pair >= d)
            def _():
                later_copy(d, odd, t).start()

        @pl.when(odd == 1)
        def _():
            state_copy(t).start()

        grad_copy(t).wait_send()

        @pl.when(t + IN_FLIGHT < chunks)
        def _():
            grad_copy(t + IN_FLIGHT).start()

    def stage_suffix(t):
        sum_s[...] = jnp.zeros(sum_s.shape, jnp.float32)
        for d in range(1, reach + 1):

            @pl.when(pair + d < pairs)
            def _():
                for sender in range(2):
                    later_copy(d, sender, t).wait_recv()
                    for u in range(CHUNK_HEADS):
                        term = later_in_s[d - 1, sender, t, u].astype(jnp.float32)
                        for b in range(1, 2 * d - 1 + sender):
                            term = term * link_s[me + b, pl.ds(t * CHUNK_HEADS + u, 1), :]
                        sum_s[u] += term

        suffix_s[t] = sum_s[...].astype(jnp.bfloat16)
        suffix_copy(t).start()

    def stage_inner(t, u):
        h = t * CHUNK_HEADS + u
        slot = lax.rem(t, SLOTS)
        q, k, v, g = (ref[t, :, part(u)] for ref in (q_s, k_s, v_s, g_s))
        row = run_s[pl.ds(h, 1), :]
        grad_q = [None] * blocks
        for block in range(blocks):
            low, high = block * LANES, (block + 1) * LANES
            wide = jnp.concatenate([col_s[h, low:high, :]] * (blocks - block), axis=1)
            weight = jnp.exp((row[:, low:] - wide) + bias_s[low:high, low:])
            scores = dot(k[low:high], q[low:], 1, 1)
            grad_dots = dot(v[low:high], g[low:], 1, 1)
            attention = (weight * scores).astype(jnp.bfloat16)
            grad_mix = (weight * grad_dots).astype(jnp.bfloat16)
            inner_s[slot, 0, low:high, part(u)] = dot(grad_mix, q[low:], 1, 0)
            inner_s[slot, 1, low:high, part(u)] = dot(attention, g[low:], 1, 0)
            spread = dot(grad_mix, k[low:high], 0, 0)
            for i in range(block, blocks):
                piece = spread[(i - block) * LANES : (i - block + 1) * LANES]
                grad_q[i] = piece if grad_q[i] is None else grad_q[i] + piece
        prefix = prefix_s[h].astype(jnp.bfloat16)
        grad_q = jnp.concatenate(grad_q, axis=0) + dot(g, prefix, 1, 1) * head_weight(h)
        out_q[:, head_columns(h)] = grad_q.astype(jnp.bfloat16)

    def stage_finish(t):
        slot = lax.rem(t, SLOTS)

        @pl.when(odd == 0)
        def _():
            state_copy(t).wait_recv()
            suffix_copy(t).wait_recv()
            for u in range(CHUNK_HEADS):
                link = link_s[me + 1, pl.ds(t * CHUNK_HEADS + u, 1), :]
                carried = link * suffix_in_s[t, u].astype(jnp.float32)
                total = odd_state_s[t, u].astype(jnp.float32) + carried
                suffix_s[t, u] = total.astype(jnp.bfloat16)

        for u in range(CHUNK_HEADS):
            h = t * CHUNK_HEADS + u
            suffix = suffix_s[t, u]
            tail = jnp.exp(col_s[h, length - 1 : length, :] - col_s[h]) * tail_mask_s[...]
            grad_k = inner_s[slot, 0, :, part(u)] + dot(v_s[t, :, part(u)], suffix, 1, 1) * tail
            grad_v = inner_s[slot, 1, :, part(u)] + dot(k_s[t, :, part(u)], suffix, 1, 0) * tail
            out_k[:, head_columns(h)] = grad_k.astype(jnp.bfloat16)
            out_v[:, head_columns(h)] = grad_v.astype(jnp.bfloat16)

    @pl.loop(0, chunks + FINISH_LAG)
    def _(step):
        @pl.when((step >= SUFFIX_LAG) & (step < chunks + SUFFIX_LAG) & (odd == 1))
        def _():
            stage_suffix(step - SUFFIX_LAG)

        @pl.when(step < chunks)
        def _():
            stage_state(step)
            load_copy(1, step).wait()
            load_copy(2, step).wait()
            for u in range(CHUNK_HEADS):
                stage_inner(step, u)

        @pl.when(step >= FINISH_LAG)
        def _():
            stage_finish(step - FINISH_LAG)

    for k in range(1, ctx_count):
        meta_copy(k).wait_send()

    @pl.loop(0, chunks)
    def _(t):
        @pl.when(odd == 1)
        def _():
            state_copy(t).wait_send()
            suffix_copy(t).wait_send()

        for d in range(1, reach + 1):

            @pl.when(pair >= d)
            def _():
                later_copy(d, odd, t).wait_send()


def place_kernel(in_q, in_k, in_v, out_q, out_k, out_v, sem):
    rows = in_q.shape[0] // PLACE_PARTS
    copies = []
    for j in range(PLACE_PARTS):
        span = slice(j * rows, (j + 1) * rows)
        for i, (source, target) in enumerate(((in_q, out_q), (in_k, out_k), (in_v, out_v))):
            copies.append(
                pltpu.make_async_copy(source.at[span], target.at[0, span], sem.at[i, j])
            )
    for copy in copies:
        copy.start()
    for copy in copies:
        copy.wait()


def solution(mesh):
    pipe_count, ctx_count = mesh.shape["pipe"], mesh.shape["ctx"]

    def on_device(queries, key_rows, value_rows, next_grads, log_decay, doc_ids, prefix_states):
        _, length, width = queries.shape
        heads = log_decay.shape[1]
        head_dim = width // heads
        chunks = heads // CHUNK_HEADS
        chunk_cols = head_dim * CHUNK_HEADS
        reach = ctx_count // 4
        any_spec = pl.BlockSpec(memory_space=pl.ANY)
        vmem_spec = pl.BlockSpec(memory_space=pltpu.VMEM)
        f32, bf16 = jnp.float32, jnp.bfloat16
        rows = pltpu.VMEM((chunks, length, chunk_cols), bf16)
        states = pltpu.VMEM((chunks, CHUNK_HEADS, head_dim, head_dim), bf16)
        mask = pltpu.VMEM((length, LANES), f32)
        dma = pltpu.SemaphoreType.DMA
        grads = pl.pallas_call(
            functools.partial(kernel, pipe_count, ctx_count),
            out_shape=[pltpu.VMEM((length, width), bf16)] * 3,
            in_specs=[any_spec] * 7,
            out_specs=[vmem_spec] * 3,
            scratch_shapes=[
                rows,
                rows,
                rows,
                rows,
                pltpu.VMEM((heads, head_dim, head_dim), f32),
                pltpu.VMEM((heads, length), f32),
                pltpu.VMEM((heads, length, LANES), f32),
                pltpu.VMEM((length, length), f32),
                mask,
                mask,
                pltpu.VMEM((heads + 16, LANES), f32),
                pltpu.VMEM((ctx_count, heads + 16, LANES), f32),
                pltpu.VMEM((ctx_count, heads, LANES), f32),
                pltpu.VMEM((ctx_count, 8, LANES), f32),
                pltpu.VMEM((heads, length), f32),
                pltpu.VMEM((1, length), jnp.int32),
                pltpu.VMEM((CHUNK_HEADS, head_dim, head_dim), f32),
                states,
                states,
                pltpu.VMEM((reach, 2, chunks, CHUNK_HEADS, head_dim, head_dim), bf16),
                states,
                states,
                pltpu.VMEM((SLOTS, 2, length, chunk_cols), f32),
                dma((3, chunks)),
                dma,
                dma((2,)),
                dma((chunks,)),
                dma((chunks,)),
                dma((ctx_count,)),
                dma((ctx_count,)),
                dma((chunks,)),
                dma((chunks,)),
                dma((reach, chunks)),
                dma((reach, 2, chunks)),
                dma((chunks,)),
                dma((chunks,)),
            ],
            compiler_params=pltpu.CompilerParams(
                collective_id=0, has_side_effects=True, vmem_limit_bytes=46 * 1024 * 1024
            ),
        )(queries, key_rows, value_rows, next_grads, log_decay, doc_ids, prefix_states)
        return pl.pallas_call(
            place_kernel,
            out_shape=[jax.ShapeDtypeStruct(queries.shape, bf16)] * 3,
            in_specs=[vmem_spec] * 3,
            out_specs=[any_spec] * 3,
            scratch_shapes=[dma((3, PLACE_PARTS))],
            compiler_params=pltpu.CompilerParams(vmem_limit_bytes=12 * 1024 * 1024),
        )(*grads)

    return jax.shard_map(
        on_device,
        mesh=mesh,
        in_specs=(
            P("pipe", "ctx", None),
            P("pipe", "ctx", None),
            P("pipe", "ctx", None),
            P("pipe", "ctx", None),
            P("pipe", None, "ctx"),
            P("pipe", "ctx"),
            P("pipe", "ctx", None, None, None),
        ),
        out_specs=(P("pipe", "ctx", None), P("pipe", "ctx", None), P("pipe", "ctx", None)),
        check_vma=False,
    )
```

```python
import functools

import jax
import jax.numpy as jnp
from jax import lax
from jax.experimental import pallas as pl
from jax.experimental.pallas import tpu as pltpu
from jax.sharding import PartitionSpec as P

MESH = pl.DeviceIdType.MESH
LANES = 128
CHUNK_HEADS = 1
IN_FLIGHT = 3
SUFFIX_LAG = 3
FINISH_LAG = 4
SLOTS = FINISH_LAG + 1
PLACE_PARTS = 8
MASKED = -1e30


def dot(a, b, a_dim, b_dim, precision=None):
    return lax.dot_general(
        a,
        b,
        (((a_dim,), (b_dim,)), ((), ())),
        precision=precision,
        preferred_element_type=jnp.float32,
    )


def as_columns(row, width):
    return jnp.broadcast_to(row, (width, row.shape[1])).T


def kernel(
    pipe_count,
    ctx_count,
    q_hbm,
    k_hbm,
    v_hbm,
    g_hbm,
    decay_hbm,
    doc_hbm,
    prefix_hbm,
    out_q,
    out_k,
    out_v,
    q_s,
    k_s,
    v_s,
    g_s,
    prefix_s,
    run_s,
    col_s,
    bias_s,
    head_mask_s,
    tail_mask_s,
    meta_own,
    meta_all,
    link_s,
    cont_s,
    decay_s,
    doc_s,
    sum_s,
    state_s,
    odd_state_s,
    later_in_s,
    suffix_s,
    suffix_in_s,
    inner_s,
    load_sem,
    prefix_sem,
    small_sem,
    g_send,
    g_recv,
    meta_send,
    meta_recv,
    state_send,
    state_recv,
    later_send,
    later_recv,
    suffix_send,
    suffix_recv,
):
    chunks, length, chunk_cols = q_s.shape
    head_dim = chunk_cols // CHUNK_HEADS
    heads = run_s.shape[0]
    blocks = length // LANES
    pairs = ctx_count // 2
    reach = ctx_count // 4
    section = lax.axis_index("pipe")
    me = lax.axis_index("ctx")
    odd = lax.rem(me, 2)
    pair = me // 2
    earlier = lax.rem(section + pipe_count - 1, pipe_count)
    later = lax.rem(section + 1, pipe_count)

    barrier = pltpu.get_barrier_semaphore()
    pl.semaphore_signal(barrier, inc=1, device_id={"pipe": earlier}, device_id_type=MESH)
    pl.semaphore_signal(barrier, inc=1, device_id={"pipe": later}, device_id_type=MESH)
    for k in range(1, ctx_count):
        pl.semaphore_signal(
            barrier, inc=1, device_id={"ctx": lax.rem(me + k, ctx_count)}, device_id_type=MESH
        )
    pl.semaphore_wait(barrier, ctx_count + 1)

    def columns(t):
        return pl.ds(pl.multiple_of(t * chunk_cols, chunk_cols), chunk_cols)

    def grad_copy(t):
        return pltpu.make_async_remote_copy(
            src_ref=g_hbm.at[0, :, columns(t)],
            dst_ref=g_s.at[t],
            send_sem=g_send.at[t],
            recv_sem=g_recv.at[t],
            device_id={"pipe": earlier},
            device_id_type=MESH,
        )

    def load_copy(i, t):
        source, target = ((q_hbm, q_s), (k_hbm, k_s), (v_hbm, v_s))[i]
        return pltpu.make_async_copy(
            source.at[0, :, columns(t)], target.at[t], load_sem.at[i, t]
        )

    def meta_copy(k):
        return pltpu.make_async_remote_copy(
            src_ref=meta_own,
            dst_ref=meta_all.at[me],
            send_sem=meta_send.at[k],
            recv_sem=meta_recv.at[k],
            device_id={"ctx": lax.rem(me + k, ctx_count)},
            device_id_type=MESH,
        )

    def meta_arrival(k):
        return pltpu.make_async_remote_copy(
            src_ref=meta_own,
            dst_ref=meta_all.at[lax.rem(me + ctx_count - k, ctx_count)],
            send_sem=meta_send.at[k],
            recv_sem=meta_recv.at[k],
            device_id={"ctx": lax.rem(me + k, ctx_count)},
            device_id_type=MESH,
        )

    partner = me + 1 - 2 * odd

    def state_copy(t):
        return pltpu.make_async_remote_copy(
            src_ref=state_s.at[t],
            dst_ref=odd_state_s.at[t],
            send_sem=state_send.at[t],
            recv_sem=state_recv.at[t],
            device_id={"ctx": partner},
            device_id_type=MESH,
        )

    def suffix_copy(t):
        return pltpu.make_async_remote_copy(
            src_ref=suffix_s.at[t],
            dst_ref=suffix_in_s.at[t],
            send_sem=suffix_send.at[t],
            recv_sem=suffix_recv.at[t],
            device_id={"ctx": partner},
            device_id_type=MESH,
        )

    def later_copy(d, sender, t):
        return pltpu.make_async_remote_copy(
            src_ref=state_s.at[t],
            dst_ref=later_in_s.at[d - 1, sender, t],
            send_sem=later_send.at[d - 1, t],
            recv_sem=later_recv.at[d - 1, sender, t],
            device_id={"ctx": lax.rem(me - odd - 2 * d + 1 + ctx_count, ctx_count)},
            device_id_type=MESH,
        )

    for t in range(IN_FLIGHT):
        grad_copy(t).start()
    decay_copy = pltpu.make_async_copy(decay_hbm.at[0], decay_s, small_sem.at[0])
    doc_copy = pltpu.make_async_copy(doc_hbm, doc_s, small_sem.at[1])
    decay_copy.start()
    doc_copy.start()

    @pl.loop(0, chunks)
    def _(t):
        for i in range(3):
            load_copy(i, t).start()

    prefix_copy = pltpu.make_async_copy(prefix_hbm.at[0, 0], prefix_s, prefix_sem)
    prefix_copy.start()

    rows = lax.broadcasted_iota(jnp.int32, (length, length), 0)
    cols = lax.broadcasted_iota(jnp.int32, (length, length), 1)
    ordered = rows <= cols
    decay_copy.wait()
    doc_copy.wait()
    running = dot(
        decay_s[...], jnp.where(ordered, 1.0, 0.0), 1, 0, precision=lax.Precision.HIGHEST
    )
    run_s[...] = running
    doc_row = doc_s[...].astype(jnp.float32)
    first_doc = jnp.broadcast_to(doc_row[:, 0:1], (8, LANES))
    last_doc = jnp.broadcast_to(doc_row[:, length - 1 : length], (8, LANES))
    meta_own[0:heads] = jnp.broadcast_to(
        jnp.exp(running[:, length - 1 : length]), (heads, LANES)
    )
    meta_own[heads : heads + 8] = first_doc
    meta_own[heads + 8 : heads + 16] = last_doc
    meta_all[me] = meta_own[...]
    for k in range(1, ctx_count):
        meta_copy(k).start()

    doc_cols = as_columns(doc_row, LANES)
    doc_wide = jnp.concatenate([doc_cols] * blocks, axis=1)
    bias_s[...] = jnp.where(ordered & (doc_wide == doc_row), 0.0, MASKED)
    tail_mask_s[...] = jnp.where(doc_cols == last_doc[0:1], 1.0, 0.0)

    @pl.loop(0, heads)
    def _(h):
        col_s[h] = as_columns(run_s[pl.ds(h, 1), :], LANES)

    for k in range(1, ctx_count):
        meta_arrival(k).wait_recv()
    for b in range(ctx_count):
        first_here = meta_all[b, heads : heads + 8]
        last_here = meta_all[b, heads + 8 : heads + 16]
        if b > 0:
            last_before = meta_all[b - 1, heads + 8 : heads + 16]
            continues = jnp.where(first_here == last_before, 1.0, 0.0)
        else:
            continues = jnp.zeros((8, LANES), jnp.float32)
        cont_s[b] = continues
        passes = jnp.where(first_here == last_here, continues, 0.0)
        link_s[b] = meta_all[b, 0:heads] * passes[0:1]
    head_mask_s[...] = jnp.where(doc_cols == first_doc[0:1], 1.0, 0.0) * cont_s[me][0:1]
    prefix_copy.wait()

    def head_columns(h):
        return pl.ds(pl.multiple_of(h * head_dim, head_dim), head_dim)

    def part(u):
        return slice(u * head_dim, (u + 1) * head_dim)

    def head_weight(h):
        return jnp.exp(col_s[h]) * head_mask_s[...]

    def stage_state(t):
        grad_copy(t).wait_recv()
        load_copy(0, t).wait()
        for u in range(CHUNK_HEADS):
            weighted = head_weight(t * CHUNK_HEADS + u) * g_s[t, :, part(u)].astype(jnp.float32)
            state = dot(q_s[t, :, part(u)], weighted.astype(jnp.bfloat16), 0, 0)
            state_s[t, u] = state.astype(jnp.bfloat16)
        for d in range(1, reach + 1):

            @pl.when(pair >= d)
            def _():
                later_copy(d, odd, t).start()

        @pl.when(odd == 1)
        def _():
            state_copy(t).start()

        grad_copy(t).wait_send()

        @pl.when(t + IN_FLIGHT < chunks)
        def _():
            grad_copy(t + IN_FLIGHT).start()

    def stage_suffix(t):
        sum_s[...] = jnp.zeros(sum_s.shape, jnp.float32)
        for d in range(1, reach + 1):

            @pl.when(pair + d < pairs)
            def _():
                for sender in range(2):
                    later_copy(d, sender, t).wait_recv()
                    for u in range(CHUNK_HEADS):
                        term = later_in_s[d - 1, sender, t, u].astype(jnp.float32)
                        for b in range(1, 2 * d - 1 + sender):
                            term = term * link_s[me + b, pl.ds(t * CHUNK_HEADS + u, 1), :]
                        sum_s[u] += term

        suffix_s[t] = sum_s[...].astype(jnp.bfloat16)
        suffix_copy(t).start()

    def stage_inner(t, u):
        h = t * CHUNK_HEADS + u
        slot = lax.rem(t, SLOTS)
        q, k, v, g = (ref[t, :, part(u)] for ref in (q_s, k_s, v_s, g_s))
        row = run_s[pl.ds(h, 1), :]
        grad_q = [None] * blocks
        for block in range(blocks):
            low, high = block * LANES, (block + 1) * LANES
            wide = jnp.concatenate([col_s[h, low:high, :]] * (blocks - block), axis=1)
            weight = jnp.exp((row[:, low:] - wide) + bias_s[low:high, low:])
            scores = dot(k[low:high], q[low:], 1, 1)
            grad_dots = dot(v[low:high], g[low:], 1, 1)
            attention = (weight * scores).astype(jnp.bfloat16)
            grad_mix = (weight * grad_dots).astype(jnp.bfloat16)
            inner_s[slot, 0, low:high, part(u)] = dot(grad_mix, q[low:], 1, 0)
            inner_s[slot, 1, low:high, part(u)] = dot(attention, g[low:], 1, 0)
            spread = dot(grad_mix, k[low:high], 0, 0)
            for i in range(block, blocks):
                piece = spread[(i - block) * LANES : (i - block + 1) * LANES]
                grad_q[i] = piece if grad_q[i] is None else grad_q[i] + piece
        prefix = prefix_s[h].astype(jnp.bfloat16)
        grad_q = jnp.concatenate(grad_q, axis=0) + dot(g, prefix, 1, 1) * head_weight(h)
        out_q[:, head_columns(h)] = grad_q.astype(jnp.bfloat16)

    def stage_finish(t):
        slot = lax.rem(t, SLOTS)

        @pl.when(odd == 0)
        def _():
            state_copy(t).wait_recv()
            suffix_copy(t).wait_recv()
            for u in range(CHUNK_HEADS):
                link = link_s[me + 1, pl.ds(t * CHUNK_HEADS + u, 1), :]
                carried = link * suffix_in_s[t, u].astype(jnp.float32)
                total = odd_state_s[t, u].astype(jnp.float32) + carried
                suffix_s[t, u] = total.astype(jnp.bfloat16)

        for u in range(CHUNK_HEADS):
            h = t * CHUNK_HEADS + u
            suffix = suffix_s[t, u]
            tail = jnp.exp(col_s[h, length - 1 : length, :] - col_s[h]) * tail_mask_s[...]
            grad_k = inner_s[slot, 0, :, part(u)] + dot(v_s[t, :, part(u)], suffix, 1, 1) * tail
            grad_v = inner_s[slot, 1, :, part(u)] + dot(k_s[t, :, part(u)], suffix, 1, 0) * tail
            out_k[:, head_columns(h)] = grad_k.astype(jnp.bfloat16)
            out_v[:, head_columns(h)] = grad_v.astype(jnp.bfloat16)

    @pl.loop(0, chunks + FINISH_LAG)
    def _(step):
        @pl.when((step >= SUFFIX_LAG) & (step < chunks + SUFFIX_LAG) & (odd == 1))
        def _():
            stage_suffix(step - SUFFIX_LAG)

        @pl.when(step < chunks)
        def _():
            stage_state(step)
            load_copy(1, step).wait()
            load_copy(2, step).wait()
            for u in range(CHUNK_HEADS):
                stage_inner(step, u)

        @pl.when(step >= FINISH_LAG)
        def _():
            stage_finish(step - FINISH_LAG)

    for k in range(1, ctx_count):
        meta_copy(k).wait_send()

    @pl.loop(0, chunks)
    def _(t):
        @pl.when(odd == 1)
        def _():
            state_copy(t).wait_send()
            suffix_copy(t).wait_send()

        for d in range(1, reach + 1):

            @pl.when(pair >= d)
            def _():
                later_copy(d, odd, t).wait_send()


def place_kernel(in_q, in_k, in_v, out_q, out_k, out_v, sem):
    rows = in_q.shape[0] // PLACE_PARTS
    copies = []
    for j in range(PLACE_PARTS):
        span = slice(j * rows, (j + 1) * rows)
        for i, (source, target) in enumerate(((in_q, out_q), (in_k, out_k), (in_v, out_v))):
            copies.append(
                pltpu.make_async_copy(source.at[span], target.at[0, span], sem.at[i, j])
            )
    for n, copy in enumerate(copies):
        copy.start(priority=n % 2)
    for copy in copies:
        copy.wait()


def solution(mesh):
    pipe_count, ctx_count = mesh.shape["pipe"], mesh.shape["ctx"]

    def on_device(queries, key_rows, value_rows, next_grads, log_decay, doc_ids, prefix_states):
        _, length, width = queries.shape
        heads = log_decay.shape[1]
        head_dim = width // heads
        chunks = heads // CHUNK_HEADS
        chunk_cols = head_dim * CHUNK_HEADS
        reach = ctx_count // 4
        any_spec = pl.BlockSpec(memory_space=pl.ANY)
        vmem_spec = pl.BlockSpec(memory_space=pltpu.VMEM)
        f32, bf16 = jnp.float32, jnp.bfloat16
        rows = pltpu.VMEM((chunks, length, chunk_cols), bf16)
        states = pltpu.VMEM((chunks, CHUNK_HEADS, head_dim, head_dim), bf16)
        mask = pltpu.VMEM((length, LANES), f32)
        dma = pltpu.SemaphoreType.DMA
        grads = pl.pallas_call(
            functools.partial(kernel, pipe_count, ctx_count),
            out_shape=[pltpu.VMEM((length, width), bf16)] * 3,
            in_specs=[any_spec] * 7,
            out_specs=[vmem_spec] * 3,
            scratch_shapes=[
                rows,
                rows,
                rows,
                rows,
                pltpu.VMEM((heads, head_dim, head_dim), f32),
                pltpu.VMEM((heads, length), f32),
                pltpu.VMEM((heads, length, LANES), f32),
                pltpu.VMEM((length, length), f32),
                mask,
                mask,
                pltpu.VMEM((heads + 16, LANES), f32),
                pltpu.VMEM((ctx_count, heads + 16, LANES), f32),
                pltpu.VMEM((ctx_count, heads, LANES), f32),
                pltpu.VMEM((ctx_count, 8, LANES), f32),
                pltpu.VMEM((heads, length), f32),
                pltpu.VMEM((1, length), jnp.int32),
                pltpu.VMEM((CHUNK_HEADS, head_dim, head_dim), f32),
                states,
                states,
                pltpu.VMEM((reach, 2, chunks, CHUNK_HEADS, head_dim, head_dim), bf16),
                states,
                states,
                pltpu.VMEM((SLOTS, 2, length, chunk_cols), f32),
                dma((3, chunks)),
                dma,
                dma((2,)),
                dma((chunks,)),
                dma((chunks,)),
                dma((ctx_count,)),
                dma((ctx_count,)),
                dma((chunks,)),
                dma((chunks,)),
                dma((reach, chunks)),
                dma((reach, 2, chunks)),
                dma((chunks,)),
                dma((chunks,)),
            ],
            compiler_params=pltpu.CompilerParams(
                collective_id=0, has_side_effects=True, vmem_limit_bytes=46 * 1024 * 1024
            ),
        )(queries, key_rows, value_rows, next_grads, log_decay, doc_ids, prefix_states)
        return pl.pallas_call(
            place_kernel,
            out_shape=[jax.ShapeDtypeStruct(queries.shape, bf16)] * 3,
            in_specs=[vmem_spec] * 3,
            out_specs=[any_spec] * 3,
            scratch_shapes=[dma((3, PLACE_PARTS))],
            compiler_params=pltpu.CompilerParams(vmem_limit_bytes=12 * 1024 * 1024),
        )(*grads)

    return jax.shard_map(
        on_device,
        mesh=mesh,
        in_specs=(
            P("pipe", "ctx", None),
            P("pipe", "ctx", None),
            P("pipe", "ctx", None),
            P("pipe", "ctx", None),
            P("pipe", None, "ctx"),
            P("pipe", "ctx"),
            P("pipe", "ctx", None, None, None),
        ),
        out_specs=(P("pipe", "ctx", None), P("pipe", "ctx", None), P("pipe", "ctx", None)),
        check_vma=False,
    )
```
